256 devices in a mesh: tm: 64 (over z, y, core), tp: 4 (over x).
Axes of the slice: x: 4, y: 4, z: 8, core: 2. Of those that a mesh axis runs over, the one named last changes fastest.
Arguments:
- starts: float32 [64, 128, 3072], P('tm', None, 'tp'), may hold values from -6 to 6
- modulation: float32 [64, 3, 3072], P('tm'), may hold values from -5 to 5
- w_qkv: bfloat16 [3072, 3, 1536], P(None, None, 'tp'), may hold values from -0.109375 to 0.109375
- norm_gain: float32 [2, 128], replicated, may hold values from 1.5 to 8
- w_out: bfloat16 [1536, 3072], P('tp'), may hold values from -0.15625 to 0.15625
- offset: int32 [1], replicated, may hold values from 0 to 128
Outputs:
- updated: float32 [64, 128, 3072], P('tm', None, 'tp')
- drift: float32 [64, 128, 3072], P('tm', None, 'tp')
- residual: float32 [64], P('tm')
The draws below stay inside these ranges and needn't reach their ends.
All inputs are finite; a program needn't handle non-finite values.
Results may differ from the reference program's by a relative error of at most 0.0018.
The reference program's roundings to bfloat16 on the way (of `modin`, `probs`, `values_bf` and `heads`) count: a program that leaves them out, or rounds other values in their place, can miss the bound.
Values may be sent and summed in bfloat16 or wider, within the bound.
A program may use at most 128 MiB of HBM per device.

```python
import jax
import jax.numpy as jnp
from jax import lax

D = 3072
HEADS = 12
HEAD = 128
L = 128
TIME = 64
STEPS = 192


def draw_norm_gain(key, part):
    key = jax.random.fold_in(key, 11)
    return jax.random.uniform(key, (2, HEAD), jnp.float32, 1.5, 2.5)


def levels(rng, extent, pieces, smallest, largest):
    level = 1.0
    for dim, blocks in pieces:
        draws = jax.random.uniform(jax.random.fold_in(jax.random.fold_in(rng, 6), dim), (blocks,), jnp.float32, smallest / len(pieces), largest / len(pieces))
        level = level * jnp.repeat(jnp.exp(draws), extent[dim] // blocks).reshape((-1,) + (1,) * (len(extent) - 1 - dim))
    return level


def bell_draw(key, shape, deviation, bound, split=(), held_as=jnp.bfloat16):
    entries = jax.random.normal(key, shape, jnp.float32) * deviation
    if len(split) > 0:
        entries = levels(key, shape, split, -0.22, 0.18) * entries
    return jnp.clip(entries, min=-bound, max=bound).astype(held_as)


def setup_inputs(seed: int = 0) -> dict:
    arg_keys = jax.random.split(jax.random.key(seed), 7)
    starts = bell_draw(arg_keys[0], (TIME, L, D), 1.0, 6.0, ((0, 64), (2, 4)), jnp.float32)
    modulation = bell_draw(arg_keys[1], (TIME, 3, D), 1.0, 5.0, ((0, 64),), jnp.float32)
    w_qkv = bell_draw(arg_keys[2], (D, 3, HEADS * HEAD), D ** -0.5, 0.109375, ((2, 4),))
    norm_gain = draw_norm_gain(jax.random.fold_in(arg_keys[6], 71), 0)
    w_out = bell_draw(arg_keys[4], (HEADS * HEAD, D), (HEADS * HEAD) ** -0.5, 0.15625, ((0, 4),))
    offset = jax.random.randint(arg_keys[5], (1,), 0, STEPS - TIME + 1).astype(jnp.int32)
    return {"starts": starts, "modulation": modulation, "w_qkv": w_qkv, "norm_gain": norm_gain, "w_out": w_out, "offset": offset}


EPSILON = 1e-06

def noise_level(position):
    fraction = 1.0 - position / STEPS
    return 3.0 * fraction / (1.0 + 2.0 * fraction)

def rms_scale(tensor, gain):
    return tensor * lax.rsqrt(lax.optimization_barrier(jnp.mean(tensor * tensor, axis=-1, keepdims=True)) + EPSILON) * gain

def reference(starts, modulation, w_qkv, norm_gain, w_out, offset):
    joined = w_qkv.reshape(D, 3 * HEADS * HEAD)

    def picard_step(running, inputs):
        latent, modulate, time_index = inputs
        row_mean = lax.optimization_barrier(jnp.mean(latent, axis=1, keepdims=True))
        centered = latent - row_mean
        row_var = lax.optimization_barrier(jnp.mean(centered * centered, axis=1, keepdims=True))
        normed = centered * lax.rsqrt(row_var + EPSILON)
        modin = (normed * (1.0 + modulate[1]) + modulate[0]).astype(jnp.bfloat16)
        projected = jnp.dot(modin, joined, preferred_element_type=jnp.float32).reshape(L, 3, HEADS, HEAD)
        queries = rms_scale(projected[:, 0], norm_gain[0])
        keys_here = rms_scale(projected[:, 1], norm_gain[1])
        scores = jnp.einsum('qhe,khe->hqk', queries, keys_here, precision=lax.Precision.HIGHEST) / jnp.sqrt(jnp.float32(HEAD))
        probs = jax.nn.softmax(scores, axis=-1).astype(jnp.bfloat16)
        values_bf = projected[:, 2].astype(jnp.bfloat16)
        probs_wide, values_wide = lax.optimization_barrier((probs, values_bf))
        heads = jnp.einsum('hqk,khe->qhe', probs_wide.astype(jnp.float32), values_wide.astype(jnp.float32))
        heads = heads.astype(jnp.bfloat16).reshape(L, HEADS * HEAD)
        attended = jnp.dot(heads, w_out, preferred_element_type=jnp.float32)
        drift = latent + modulate[2] * attended
        position = (offset[0] + time_index).astype(jnp.float32)
        step_size = noise_level(position + 1.0) - noise_level(position)
        new_end = running + step_size * drift
        change = running - latent
        residual_value = jnp.mean(change * change)
        return (new_end, (new_end, drift, residual_value))
    indices = jnp.arange(TIME, dtype=jnp.int32)
    final, outputs = lax.scan(picard_step, starts[0], (starts, modulation, indices))
    return (outputs[0], outputs[1], outputs[2])
```

```python
import functools

import jax
import jax.numpy as jnp
from jax import lax
from jax.experimental import pallas as pl
from jax.experimental.pallas import tpu as pltpu
from jax.sharding import PartitionSpec as P

HEAD = 128
EPSILON = 1e-06
MESH = pl.DeviceIdType.MESH

NX = 4
NQ = 8
NZ = 8
PARTS = 2


class Copies:
    def __init__(self, send, recv):
        self.send, self.recv, self.used = send, recv, 0

    def remote(self, src, dst, device):
        at = self.used
        self.used += 1
        return pltpu.make_async_remote_copy(
            src_ref=src,
            dst_ref=dst,
            send_sem=self.send.at[at],
            recv_sem=self.recv.at[at],
            device_id=device,
            device_id_type=MESH,
        )


REMOTE = 3 + 3 + 7 + 7 + 7 + PARTS * (3 + 7 + 7 + 7) + 3


def kernel(
    starts_hbm, mod_hbm, wq_hbm, gain_ref, wo_hbm, off_ref,
    upd_hbm, drift_hbm, res_ref,
    lat, mod, wq, wo, st, xin, acc, heads, psend, precv, s0p, s0,
    csend, arecv, bsend, brecv, csum, esend, erecv, cown, drift, upd, rs,
    local_sem, send_sem, recv_sem,
):
    tokens, cols = lat.shape
    half = cols // PARTS
    rows = tokens // NQ
    tm = lax.axis_index("tm")
    x = lax.axis_index("tp")
    z = tm // NQ
    q = tm % NQ
    cp = Copies(send_sem, recv_sem)

    def xpeer(d):
        return (tm, lax.rem(x + d, NX))

    def qpeer(r):
        return (z * NQ + lax.rem(q + r, NQ), x)

    def zpeer(r):
        return (lax.rem(z + r, NZ) * NQ + q, x)

    barrier = pltpu.get_barrier_semaphore()
    for d in range(1, NX):
        pl.semaphore_signal(barrier, inc=1, device_id=xpeer(d), device_id_type=MESH)
    for r in range(1, NQ):
        pl.semaphore_signal(barrier, inc=1, device_id=qpeer(r), device_id_type=MESH)
    for r in range(1, NZ):
        pl.semaphore_signal(barrier, inc=1, device_id=zpeer(r), device_id_type=MESH)

    load_lat = pltpu.make_async_copy(starts_hbm, lat, local_sem.at[0])
    load_lat.start()
    own = pl.ds(pl.multiple_of(x * cols, cols), cols)
    load_mod = pltpu.make_async_copy(mod_hbm.at[:, :, own], mod, local_sem.at[1])
    load_mod.start()
    load_wq, load_wo = [], []
    for d in range(NX):
        block = pl.ds(pl.multiple_of(lax.rem(x + d, NX) * cols, cols), cols)
        load_wq.append(
            pltpu.make_async_copy(wq_hbm.at[:, block, :], wq.at[d], local_sem.at[2 + d])
        )
    for d in range(NX):
        block = pl.ds(pl.multiple_of(lax.rem(x + d, NX) * cols, cols), cols)
        load_wo.append(
            pltpu.make_async_copy(wo_hbm.at[:, block], wo.at[d], local_sem.at[6 + d])
        )
    for load in load_wq + load_wo:
        load.start()

    load_lat.wait()
    latent = lat[...]
    mean_here = jnp.mean(latent, axis=1, keepdims=True)
    away = latent - mean_here
    square_here = jnp.sum(away * away, axis=1, keepdims=True)
    lane = lax.broadcasted_iota(jnp.int32, (tokens, 128), 1)
    packed = jnp.where(lane == 0, mean_here, jnp.where(lane == 1, square_here, 0.0))
    st[0] = jnp.transpose(packed)[0:8, :]

    pl.semaphore_wait(barrier, (NX - 1) + (NQ - 1) + (NZ - 1))

    stat_copies = [cp.remote(st.at[0], st.at[NX - d], xpeer(d)) for d in range(1, NX)]
    for c in stat_copies:
        c.start()

    s0_a = [
        cp.remote(
            lat.at[pl.ds(pl.multiple_of(lax.rem(q + r, NQ) * rows, rows), rows), :], s0p, qpeer(r)
        )
        for r in range(1, NQ)
    ]

    @pl.when(tm == 0)
    def _():
        for c in s0_a:
            c.start()
        s0p[...] = lat[0:rows, :]

    for c in stat_copies:
        c.wait_recv()
    stats = [st[d] for d in range(NX)]
    mean_row = (stats[0][0:1] + stats[1][0:1] + stats[2][0:1] + stats[3][0:1]) / NX
    square_row = jnp.zeros_like(mean_row)
    for d in range(NX):
        shift = stats[d][0:1] - mean_row
        square_row += stats[d][1:2] + cols * (shift * shift)
    scale_row = lax.rsqrt(square_row / (cols * NX) + EPSILON)
    sub = lax.broadcasted_iota(jnp.int32, (128, tokens), 0)
    columns = jnp.transpose(jnp.where(sub == 0, mean_row, jnp.where(sub == 1, scale_row, 0.0)))
    mean_col, scale_col = columns[:, 0:1], columns[:, 1:2]
    load_mod.wait()
    normed = (lat[...] - mean_col) * scale_col
    xin[0] = (normed * (1.0 + mod[1]) + mod[0]).astype(jnp.bfloat16)

    in_copies = {d: cp.remote(xin.at[0], xin.at[NX - d], xpeer(d)) for d in (2, 1, 3)}
    for d in (2, 1, 3):
        in_copies[d].start()

    s0_b = [cp.remote(s0p, s0p, zpeer(r)) for r in range(1, NZ)]

    @pl.when(z == 0)
    def _():
        for i, c in enumerate(s0_a):

            @pl.when(q == i + 1)
            def _():
                c.wait_recv()

        for c in s0_b:
            c.start()

    def project(d, first):
        for j in range(3):
            part = jnp.dot(xin[d], wq[d, j], preferred_element_type=jnp.float32)
            acc[j] = part if first else acc[j] + part

    load_wq[0].wait()
    project(0, True)
    for d in (1, 3, 2):
        load_wq[d].wait()
        in_copies[NX - d].wait_recv()
        project(d, False)

    for h in range(acc.shape[2] // HEAD):
        here = slice(h * HEAD, (h + 1) * HEAD)

        def normal(j):
            t = acc[j, :, here]
            scale = lax.rsqrt(jnp.mean(t * t, axis=-1, keepdims=True) + EPSILON)
            return t * scale * gain_ref[j : j + 1, :]

        scores = lax.dot_general(
            normal(0), normal(1), (((1,), (1,)), ((), ())),
            precision=lax.Precision.HIGHEST, preferred_element_type=jnp.float32,
        ) * (HEAD ** -0.5)
        top = jnp.max(scores, axis=-1, keepdims=True)
        weight = jnp.exp(scores - top)
        probs = (weight / jnp.sum(weight, axis=-1, keepdims=True)).astype(jnp.bfloat16)
        values = acc[2, :, here].astype(jnp.bfloat16)
        heads[:, here] = jnp.dot(probs, values, preferred_element_type=jnp.float32).astype(
            jnp.bfloat16
        )

    for load in load_wo:
        load.wait()
    part_copies = []
    for p in range(PARTS):
        at = slice(p * half, (p + 1) * half)
        copies = {}
        for d in (2, 1, 3):
            psend[p, d] = jnp.dot(
                heads[...], wo[d, :, at], preferred_element_type=jnp.float32
            ).astype(jnp.bfloat16)
            copies[d] = cp.remote(psend.at[p, d], precv.at[p, NX - d], xpeer(d))
            copies[d].start()
        part_copies.append(copies)

    @pl.when(z != 0)
    def _():
        for i, c in enumerate(s0_b):

            @pl.when(z == i + 1)
            def _():
                c.wait_recv()

    mine = pl.ds(pl.multiple_of(q * rows, rows), rows)
    s0_c = [cp.remote(s0p, s0.at[mine, :], qpeer(r)) for r in range(1, NQ)]
    for c in s0_c:
        c.start()
    s0[mine, :] = s0p[...]

    position = (off_ref[0] + tm).astype(jnp.float32)

    def noise_level(at):
        fraction = 1.0 - jnp.full((8, 128), at, jnp.float32) / (3.0 * NQ * NZ)
        return 3.0 * fraction / (1.0 + 2.0 * fraction)

    step_size = (noise_level(position + 1.0) - noise_level(position))[0:1, 0:1]

    a_copies, out_copies = [], []
    for p in range(PARTS):
        at = slice(p * half, (p + 1) * half)
        attended = jnp.dot(heads[...], wo[0, :, at], preferred_element_type=jnp.float32)
        for d in (1, 3, 2):
            part_copies[p][NX - d].wait_recv()
            attended += precv[p, d].astype(jnp.float32)
        drift_here = lat[:, at] + mod[2][:, at] * attended
        drift[p] = drift_here
        c_here = step_size * drift_here
        cown[p] = c_here
        csend[p] = c_here.astype(jnp.bfloat16)
        copies = []
        for r in range(1, NQ):
            there = pl.ds(pl.multiple_of(lax.rem(q + r, NQ) * rows, rows), rows)
            copies.append(cp.remote(csend.at[p, there, :], arecv.at[p, q], qpeer(r)))
            copies[-1].start()
        arecv[p, q] = csend[p, mine, :]
        a_copies.append(copies)
        out_copies.append(
            pltpu.make_async_copy(drift.at[p], drift_hbm.at[:, at], local_sem.at[10 + p])
        )
        out_copies[-1].start()

    b_copies = []
    for p in range(PARTS):
        for c in a_copies[p]:
            c.wait_recv()
        total = jnp.zeros((rows, half), jnp.float32)
        for i in range(NQ):
            csum[p, i] = total
            total += arecv[p, i].astype(jnp.float32)
        bsend[p] = total.astype(jnp.bfloat16)
        copies = []
        for r in range(1, NZ):
            copies.append(cp.remote(bsend.at[p], brecv.at[p, r], zpeer(r)))

            @pl.when(z + r < NZ)
            def _():
                copies[-1].start()

        b_copies.append(copies)

    c_copies = []
    for p in range(PARTS):
        upd[p] = jnp.zeros((tokens, half), jnp.float32)
        for r in range(1, NZ):

            @pl.when(z >= r)
            def _():
                b_copies[p][r - 1].wait_recv()
                upd[p, 0:rows, :] += brecv[p, r].astype(jnp.float32)

        before = upd[p, 0:rows, :]
        for i in range(NQ):
            esend[p, i] = (before + csum[p, i]).astype(jnp.bfloat16)
        copies = []
        for r in range(1, NQ):
            copies.append(
                cp.remote(esend.at[p, lax.rem(q + r, NQ)], erecv.at[p, mine, :], qpeer(r))
            )
            copies[-1].start()
        erecv[p, mine, :] = esend[p, q]
        c_copies.append(copies)

    for c in s0_c:
        c.wait_recv()
    squared = jnp.zeros((1, 1), jnp.float32)
    for p in range(PARTS):
        at = slice(p * half, (p + 1) * half)
        for c in c_copies[p]:
            c.wait_recv()
        fresh = s0[:, at] + erecv[p].astype(jnp.float32)
        upd[p] = fresh + cown[p]
        out_copies.append(
            pltpu.make_async_copy(upd.at[p], upd_hbm.at[:, at], local_sem.at[12 + p])
        )
        out_copies[-1].start()
        change = fresh - lat[:, at]
        squared += jnp.sum(jnp.sum(change * change, axis=1, keepdims=True), axis=0, keepdims=True)
    rs[0] = jnp.broadcast_to(squared, (8, 128))
    r_copies = [cp.remote(rs.at[0], rs.at[NX - d], xpeer(d)) for d in range(1, NX)]
    for c in r_copies:
        c.start()
    for c in r_copies:
        c.wait_recv()
    res_ref[...] = (rs[0] + rs[1] + rs[2] + rs[3]) / (tokens * cols * NX)

    for c in out_copies:
        c.wait()
    sent = stat_copies + list(in_copies.values()) + s0_c + r_copies
    for copies in part_copies:
        sent += list(copies.values())
    for copies in a_copies + c_copies:
        sent += copies
    for c in sent:
        c.wait_send()

    @pl.when(tm == 0)
    def _():
        for c in s0_a:
            c.wait_send()

    @pl.when(z == 0)
    def _():
        for c in s0_b:
            c.wait_send()

    for r in range(1, NZ):

        @pl.when(z + r < NZ)
        def _():
            for p in range(PARTS):
                b_copies[p][r - 1].wait_send()


def body(starts, modulation, w_qkv, norm_gain, w_out, offset):
    tokens, cols = starts.shape[1:]
    inner = w_out.shape[0]
    half = cols // PARTS
    rows = tokens // NQ
    f32, bf16 = jnp.float32, jnp.bfloat16
    hbm = pl.BlockSpec(memory_space=pl.ANY)
    vmem = pl.BlockSpec(memory_space=pltpu.VMEM)
    updated, drift, residual = pl.pallas_call(
        kernel,
        out_shape=(
            jax.ShapeDtypeStruct((tokens, cols), f32),
            jax.ShapeDtypeStruct((tokens, cols), f32),
            jax.ShapeDtypeStruct((8, 128), f32),
        ),
        in_specs=[hbm, hbm, hbm, vmem, hbm, pl.BlockSpec(memory_space=pltpu.SMEM)],
        out_specs=(hbm, hbm, vmem),
        scratch_shapes=[
            pltpu.VMEM((tokens, cols), f32),
            pltpu.VMEM((3, 1, cols), f32),
            pltpu.VMEM((NX, 3, cols, inner), bf16),
            pltpu.VMEM((NX, inner, cols), bf16),
            pltpu.VMEM((NX, 8, 128), f32),
            pltpu.VMEM((NX, tokens, cols), bf16),
            pltpu.VMEM((3, tokens, inner), f32),
            pltpu.VMEM((tokens, inner), bf16),
            pltpu.VMEM((PARTS, NX, tokens, half), bf16),
            pltpu.VMEM((PARTS, NX, tokens, half), bf16),
            pltpu.VMEM((rows, cols), f32),
            pltpu.VMEM((tokens, cols), f32),
            pltpu.VMEM((PARTS, tokens, half), bf16),
            pltpu.VMEM((PARTS, NQ, rows, half), bf16),
            pltpu.VMEM((PARTS, rows, half), bf16),
            pltpu.VMEM((PARTS, NZ, rows, half), bf16),
            pltpu.VMEM((PARTS, NQ, rows, half), f32),
            pltpu.VMEM((PARTS, NQ, rows, half), bf16),
            pltpu.VMEM((PARTS, tokens, half), bf16),
            pltpu.VMEM((PARTS, tokens, half), f32),
            pltpu.VMEM((PARTS, tokens, half), f32),
            pltpu.VMEM((PARTS, tokens, half), f32),
            pltpu.VMEM((NX, 8, 128), f32),
            pltpu.SemaphoreType.DMA((14,)),
            pltpu.SemaphoreType.DMA((REMOTE,)),
            pltpu.SemaphoreType.DMA((REMOTE,)),
        ],
        compiler_params=pltpu.CompilerParams(
            collective_id=0, has_side_effects=True, vmem_limit_bytes=40 * 1024 * 1024
        ),
        name="sweep",
    )(
        starts.reshape(tokens, cols),
        modulation.transpose(1, 0, 2),
        w_qkv.transpose(1, 0, 2),
        norm_gain,
        w_out,
        offset,
    )
    return (updated[None], drift[None], residual[0, 0:1])


def solution(mesh):
    in_specs = (
        P("tm", None, "tp"),
        P("tm", None, None),
        P(None, None, "tp"),
        P(),
        P("tp", None),
        P(),
    )
    out_specs = (P("tm", None, "tp"), P("tm", None, "tp"), P("tm"))
    return jax.shard_map(body, mesh=mesh, in_specs=in_specs, out_specs=out_specs, check_vma=False)
```

```python
import functools

import jax
import jax.numpy as jnp
from jax import lax
from jax.experimental import pallas as pl
from jax.experimental.pallas import tpu as pltpu
from jax.sharding import PartitionSpec as P

HEAD = 128
EPSILON = 1e-06
MESH = pl.DeviceIdType.MESH

NX = 4
NQ = 8
NZ = 8
PARTS = 2


class Copies:
    def __init__(self, send, recv):
        self.send, self.recv, self.used = send, recv, 0

    def remote(self, src, dst, device):
        at = self.used
        self.used += 1
        return pltpu.make_async_remote_copy(
            src_ref=src,
            dst_ref=dst,
            send_sem=self.send.at[at],
            recv_sem=self.recv.at[at],
            device_id=device,
            device_id_type=MESH,
        )


REMOTE = 3 + 3 + 7 + 7 + 7 + PARTS * (3 + 7 + 7 + 7) + 3


def kernel(
    starts_hbm, mod_hbm, wq_hbm, gain_ref, wo_hbm, off_ref,
    upd_hbm, drift_hbm, res_ref,
    lat, mod, wq, wo, st, xin, acc, heads, psend, precv, s0p, s0,
    csend, arecv, bsend, brecv, csum, esend, erecv, cown, drift, upd, rs,
    local_sem, send_sem, recv_sem,
):
    tokens, cols = lat.shape
    half = cols // PARTS
    rows = tokens // NQ
    tm = lax.axis_index("tm")
    x = lax.axis_index("tp")
    z = tm // NQ
    q = tm % NQ
    cp = Copies(send_sem, recv_sem)

    def xpeer(d):
        return (tm, lax.rem(x + d, NX))

    def qpeer(r):
        return (z * NQ + lax.rem(q + r, NQ), x)

    def zpeer(r):
        return (lax.rem(z + r, NZ) * NQ + q, x)

    barrier = pltpu.get_barrier_semaphore()
    for d in range(1, NX):
        pl.semaphore_signal(barrier, inc=1, device_id=xpeer(d), device_id_type=MESH)
    for r in range(1, NQ):
        pl.semaphore_signal(barrier, inc=1, device_id=qpeer(r), device_id_type=MESH)
    for r in range(1, NZ):
        pl.semaphore_signal(barrier, inc=1, device_id=zpeer(r), device_id_type=MESH)

    load_lat = pltpu.make_async_copy(starts_hbm, lat, local_sem.at[0])
    load_lat.start()
    own = pl.ds(pl.multiple_of(x * cols, cols), cols)
    load_mod = pltpu.make_async_copy(mod_hbm.at[:, :, own], mod, local_sem.at[1])
    load_mod.start()
    load_wq, load_wo = [], []
    for d in range(NX):
        block = pl.ds(pl.multiple_of(lax.rem(x + d, NX) * cols, cols), cols)
        load_wq.append(
            pltpu.make_async_copy(wq_hbm.at[:, block, :], wq.at[d], local_sem.at[2 + d])
        )
    for d in range(NX):
        block = pl.ds(pl.multiple_of(lax.rem(x + d, NX) * cols, cols), cols)
        load_wo.append(
            pltpu.make_async_copy(wo_hbm.at[:, block], wo.at[d], local_sem.at[6 + d])
        )
    for load in load_wq + load_wo:
        load.start()

    load_lat.wait()
    latent = lat[...]
    mean_here = jnp.mean(latent, axis=1, keepdims=True)
    away = latent - mean_here
    square_here = jnp.sum(away * away, axis=1, keepdims=True)
    lane = lax.broadcasted_iota(jnp.int32, (tokens, 128), 1)
    packed = jnp.where(lane == 0, mean_here, jnp.where(lane == 1, square_here, 0.0))
    st[0] = jnp.transpose(packed)[0:8, :]

    pl.semaphore_wait(barrier, (NX - 1) + (NQ - 1) + (NZ - 1))

    stat_copies = [cp.remote(st.at[0], st.at[NX - d], xpeer(d)) for d in range(1, NX)]
    for c in stat_copies:
        c.start()

    s0_a = [
        cp.remote(
            lat.at[pl.ds(pl.multiple_of(lax.rem(q + r, NQ) * rows, rows), rows), :], s0p, qpeer(r)
        )
        for r in range(1, NQ)
    ]

    @pl.when(tm == 0)
    def _():
        for c in s0_a:
            c.start()
        s0p[...] = lat[0:rows, :]

    for c in stat_copies:
        c.wait_recv()
    stats = [st[d] for d in range(NX)]
    mean_row = (stats[0][0:1] + stats[1][0:1] + stats[2][0:1] + stats[3][0:1]) / NX
    square_row = jnp.zeros_like(mean_row)
    for d in range(NX):
        shift = stats[d][0:1] - mean_row
        square_row += stats[d][1:2] + cols * (shift * shift)
    scale_row = lax.rsqrt(square_row / (cols * NX) + EPSILON)
    sub = lax.broadcasted_iota(jnp.int32, (128, tokens), 0)
    columns = jnp.transpose(jnp.where(sub == 0, mean_row, jnp.where(sub == 1, scale_row, 0.0)))
    mean_col, scale_col = columns[:, 0:1], columns[:, 1:2]
    load_mod.wait()
    normed = (lat[...] - mean_col) * scale_col
    xin[0] = (normed * (1.0 + mod[1]) + mod[0]).astype(jnp.bfloat16)

    in_copies = {d: cp.remote(xin.at[0], xin.at[NX - d], xpeer(d)) for d in (2, 1, 3)}
    for d in (2, 1, 3):
        in_copies[d].start()

    s0_b = [cp.remote(s0p, s0p, zpeer(r)) for r in range(1, NZ)]

    @pl.when(z == 0)
    def _():
        for i, c in enumerate(s0_a):

            @pl.when(q == i + 1)
            def _():
                c.wait_recv()

        for c in s0_b:
            c.start()

    def project(d, first):
        for j in range(3):
            part = jnp.dot(xin[d], wq[d, j], preferred_element_type=jnp.float32)
            acc[j] = part if first else acc[j] + part

    load_wq[0].wait()
    project(0, True)
    for d in (1, 3, 2):
        load_wq[d].wait()
        in_copies[NX - d].wait_recv()
        project(d, False)

    for h in range(acc.shape[2] // HEAD):
        here = slice(h * HEAD, (h + 1) * HEAD)

        def normal(j):
            t = acc[j, :, here]
            scale = lax.rsqrt(jnp.mean(t * t, axis=-1, keepdims=True) + EPSILON)
            return t * scale * gain_ref[j : j + 1, :]

        scores = lax.dot_general(
            normal(0), normal(1), (((1,), (1,)), ((), ())),
            precision=lax.Precision.HIGHEST, preferred_element_type=jnp.float32,
        ) * (HEAD ** -0.5)
        top = jnp.max(scores, axis=-1, keepdims=True)
        weight = jnp.exp(scores - top)
        probs = (weight / jnp.sum(weight, axis=-1, keepdims=True)).astype(jnp.bfloat16)
        values = acc[2, :, here].astype(jnp.bfloat16)
        heads[:, here] = jnp.dot(probs, values, preferred_element_type=jnp.float32).astype(
            jnp.bfloat16
        )

    for load in load_wo:
        load.wait()
    part_copies = []
    for p in range(PARTS):
        at = slice(p * half, (p + 1) * half)
        copies = {}
        for d in (2, 1, 3):
            psend[p, d] = jnp.dot(
                heads[...], wo[d, :, at], preferred_element_type=jnp.float32
            ).astype(jnp.bfloat16)
            copies[d] = cp.remote(psend.at[p, d], precv.at[p, NX - d], xpeer(d))
            copies[d].start()
        part_copies.append(copies)

    @pl.when(z != 0)
    def _():
        for i, c in enumerate(s0_b):

            @pl.when(z == i + 1)
            def _():
                c.wait_recv()

    mine = pl.ds(pl.multiple_of(q * rows, rows), rows)
    s0_c = [cp.remote(s0p, s0.at[mine, :], qpeer(r)) for r in range(1, NQ)]
    for c in s0_c:
        c.start()
    s0[mine, :] = s0p[...]

    position = (off_ref[0] + tm).astype(jnp.float32)

    def noise_level(at):
        fraction = 1.0 - jnp.full((8, 128), at, jnp.float32) / (3.0 * NQ * NZ)
        return 3.0 * fraction / (1.0 + 2.0 * fraction)

    step_size = (noise_level(position + 1.0) - noise_level(position))[0:1, 0:1]

    a_copies, out_copies = [], []
    for p in range(PARTS):
        at = slice(p * half, (p + 1) * half)
        attended = jnp.dot(heads[...], wo[0, :, at], preferred_element_type=jnp.float32)
        for d in (1, 3, 2):
            part_copies[p][NX - d].wait_recv()
            attended += precv[p, d].astype(jnp.float32)
        drift_here = lat[:, at] + mod[2][:, at] * attended
        drift[p] = drift_here
        c_here = step_size * drift_here
        cown[p] = c_here
        csend[p] = c_here.astype(jnp.bfloat16)
        copies = []
        for r in range(1, NQ):
            there = pl.ds(pl.multiple_of(lax.rem(q + r, NQ) * rows, rows), rows)
            copies.append(cp.remote(csend.at[p, there, :], arecv.at[p, q], qpeer(r)))
            copies[-1].start()
        arecv[p, q] = csend[p, mine, :]
        a_copies.append(copies)
        out_copies.append(
            pltpu.make_async_copy(drift.at[p], drift_hbm.at[:, at], local_sem.at[10 + p])
        )
        out_copies[-1].start()

    b_copies = []
    for p in range(PARTS):
        for c in a_copies[p]:
            c.wait_recv()
        total = jnp.zeros((rows, half), jnp.float32)
        for i in range(NQ):
            csum[p, i] = total
            total += arecv[p, i].astype(jnp.float32)
        bsend[p] = total.astype(jnp.bfloat16)
        copies = []
        for r in range(1, NZ):
            copies.append(cp.remote(bsend.at[p], brecv.at[p, r], zpeer(r)))

            @pl.when(z + r < NZ)
            def _():
                copies[-1].start()

        b_copies.append(copies)

    c_copies = []
    for p in range(PARTS):
        upd[p] = jnp.zeros((tokens, half), jnp.float32)
        for r in range(1, NZ):

            @pl.when(z >= r)
            def _():
                b_copies[p][r - 1].wait_recv()
                upd[p, 0:rows, :] += brecv[p, r].astype(jnp.float32)

        before = upd[p, 0:rows, :]
        for i in range(NQ):
            esend[p, i] = (before + csum[p, i]).astype(jnp.bfloat16)
        copies = []
        for r in range(1, NQ):
            copies.append(
                cp.remote(esend.at[p, lax.rem(q + r, NQ)], erecv.at[p, mine, :], qpeer(r))
            )
            copies[-1].start()
        erecv[p, mine, :] = esend[p, q]
        c_copies.append(copies)

    for c in s0_c:
        c.wait_recv()
    squared = jnp.zeros((1, 1), jnp.float32)
    for p in range(PARTS):
        at = slice(p * half, (p + 1) * half)
        for c in c_copies[p]:
            c.wait_recv()
        fresh = s0[:, at] + erecv[p].astype(jnp.float32)
        upd[p] = fresh + cown[p]
        out_copies.append(
            pltpu.make_async_copy(upd.at[p], upd_hbm.at[:, at], local_sem.at[12 + p])
        )
        out_copies[-1].start()
        change = fresh - lat[:, at]
        squared += jnp.sum(jnp.sum(change * change, axis=1, keepdims=True), axis=0, keepdims=True)
    rs[0] = jnp.broadcast_to(squared, (8, 128))
    r_copies = [cp.remote(rs.at[0], rs.at[NX - d], xpeer(d)) for d in range(1, NX)]
    for c in r_copies:
        c.start()
    for c in r_copies:
        c.wait_recv()
    res_ref[...] = (rs[0] + rs[1] + rs[2] + rs[3]) / (tokens * cols * NX)

    for c in out_copies:
        c.wait()
    sent = stat_copies + list(in_copies.values()) + s0_c + r_copies
    for copies in part_copies:
        sent += list(copies.values())
    for copies in a_copies + c_copies:
        sent += copies
    for c in sent:
        c.wait_send()

    @pl.when(tm == 0)
    def _():
        for c in s0_a:
            c.wait_send()

    @pl.when(z == 0)
    def _():
        for c in s0_b:
            c.wait_send()

    for r in range(1, NZ):

        @pl.when(z + r < NZ)
        def _():
            for p in range(PARTS):
                b_copies[p][r - 1].wait_send()


def body(starts, modulation, w_qkv, norm_gain, w_out, offset):
    tokens, cols = starts.shape[1:]
    inner = w_out.shape[0]
    half = cols // PARTS
    rows = tokens // NQ
    f32, bf16 = jnp.float32, jnp.bfloat16
    hbm = pl.BlockSpec(memory_space=pltpu.HBM)
    vmem = pl.BlockSpec(memory_space=pltpu.VMEM)
    updated, drift, residual = pl.pallas_call(
        kernel,
        out_shape=(
            jax.ShapeDtypeStruct((tokens, cols), f32),
            jax.ShapeDtypeStruct((tokens, cols), f32),
            jax.ShapeDtypeStruct((8, 128), f32),
        ),
        in_specs=[hbm, hbm, hbm, vmem, hbm, pl.BlockSpec(memory_space=pltpu.SMEM)],
        out_specs=(hbm, hbm, vmem),
        scratch_shapes=[
            pltpu.VMEM((tokens, cols), f32),
            pltpu.VMEM((3, 1, cols), f32),
            pltpu.VMEM((NX, 3, cols, inner), bf16),
            pltpu.VMEM((NX, inner, cols), bf16),
            pltpu.VMEM((NX, 8, 128), f32),
            pltpu.VMEM((NX, tokens, cols), bf16),
            pltpu.VMEM((3, tokens, inner), f32),
            pltpu.VMEM((tokens, inner), bf16),
            pltpu.VMEM((PARTS, NX, tokens, half), bf16),
            pltpu.VMEM((PARTS, NX, tokens, half), bf16),
            pltpu.VMEM((rows, cols), f32),
            pltpu.VMEM((tokens, cols), f32),
            pltpu.VMEM((PARTS, tokens, half), bf16),
            pltpu.VMEM((PARTS, NQ, rows, half), bf16),
            pltpu.VMEM((PARTS, rows, half), bf16),
            pltpu.VMEM((PARTS, NZ, rows, half), bf16),
            pltpu.VMEM((PARTS, NQ, rows, half), f32),
            pltpu.VMEM((PARTS, NQ, rows, half), bf16),
            pltpu.VMEM((PARTS, tokens, half), bf16),
            pltpu.VMEM((PARTS, tokens, half), f32),
            pltpu.VMEM((PARTS, tokens, half), f32),
            pltpu.VMEM((PARTS, tokens, half), f32),
            pltpu.VMEM((NX, 8, 128), f32),
            pltpu.SemaphoreType.DMA((14,)),
            pltpu.SemaphoreType.DMA((REMOTE,)),
            pltpu.SemaphoreType.DMA((REMOTE,)),
        ],
        compiler_params=pltpu.CompilerParams(
            collective_id=0, has_side_effects=True, vmem_limit_bytes=60 * 1024 * 1024
        ),
        name="sweep",
    )(
        starts.reshape(tokens, cols),
        modulation.transpose(1, 0, 2),
        w_qkv.transpose(1, 0, 2),
        norm_gain,
        w_out,
        offset,
    )
    return (updated[None], drift[None], residual[0, 0:1])


def solution(mesh):
    in_specs = (
        P("tm", None, "tp"),
        P("tm", None, None),
        P(None, None, "tp"),
        P(),
        P("tp", None),
        P(),
    )
    out_specs = (P("tm", None, "tp"), P("tm", None, "tp"), P("tm"))
    return jax.shard_map(body, mesh=mesh, in_specs=in_specs, out_specs=out_specs, check_vma=False)
```

```python
import functools

import jax
import jax.numpy as jnp
from jax import lax
from jax.experimental import pallas as pl
from jax.experimental.pallas import tpu as pltpu
from jax.sharding import PartitionSpec as P

HEAD = 128
EPSILON = 1e-06
MESH = pl.DeviceIdType.MESH

NX = 4
NQ = 8
NZ = 8
PARTS = 2


class Copies:
    def __init__(self, send, recv):
        self.send, self.recv, self.used = send, recv, 0

    def remote(self, src, dst, device):
        at = self.used
        self.used += 1
        return pltpu.make_async_remote_copy(
            src_ref=src,
            dst_ref=dst,
            send_sem=self.send.at[at],
            recv_sem=self.recv.at[at],
            device_id=device,
            device_id_type=MESH,
        )


REMOTE = 3 + 6 + 7 + 7 + 7 + 7 + PARTS * (3 + 7 + 7 + 7) + 31


def kernel(
    starts_hbm, mod_hbm, wq_hbm, gain_ref, wo_hbm, off_ref,
    upd_ref, drift_ref, res_ref,
    lat, mod, wq, wo, st, xin, acc, heads, psend, precv, s0p, s0,
    csend, arecv, bsend, brecv, csum, esend, erecv, cown, zsum, latp, rsend, rrecv,
    local_sem, send_sem, recv_sem,
):
    tokens, cols = lat.shape
    half = cols // PARTS
    rows = tokens // NQ
    tm = lax.axis_index("tm")
    x = lax.axis_index("tp")
    z = tm // NQ
    q = tm % NQ
    cp = Copies(send_sem, recv_sem)

    def xpeer(d):
        return (tm, lax.rem(x + d, NX))

    def qpeer(r):
        return (z * NQ + lax.rem(q + r, NQ), x)

    def xqpeer(d, r):
        return (z * NQ + lax.rem(q + r, NQ), lax.rem(x + d, NX))

    def zpeer(r):
        return (lax.rem(z + r, NZ) * NQ + q, x)

    near = [(d, r) for d in range(NX) for r in range(NQ) if d or r]
    barrier = pltpu.get_barrier_semaphore()
    for d, r in near:
        pl.semaphore_signal(barrier, inc=1, device_id=xqpeer(d, r), device_id_type=MESH)
    for r in range(1, NZ):
        pl.semaphore_signal(barrier, inc=1, device_id=zpeer(r), device_id_type=MESH)

    load_lat = pltpu.make_async_copy(starts_hbm, lat, local_sem.at[0])
    load_lat.start()
    own = pl.ds(pl.multiple_of(x * cols, cols), cols)
    load_mod = pltpu.make_async_copy(mod_hbm.at[:, :, own], mod, local_sem.at[1])
    load_mod.start()
    load_wq, load_wo = [], []
    for d in range(NX):
        block = pl.ds(pl.multiple_of(lax.rem(x + d, NX) * cols, cols), cols)
        load_wq.append(
            pltpu.make_async_copy(wq_hbm.at[:, block, :], wq.at[d], local_sem.at[2 + d])
        )
    for d in range(NX):
        block = pl.ds(pl.multiple_of(lax.rem(x + d, NX) * cols, cols), cols)
        load_wo.append(
            pltpu.make_async_copy(wo_hbm.at[:, block], wo.at[d], local_sem.at[6 + d])
        )
    for load in load_wq + load_wo:
        load.start()

    load_lat.wait()
    latent = lat[...]
    mean_here = jnp.mean(latent, axis=1, keepdims=True)
    away = latent - mean_here
    square_here = jnp.sum(away * away, axis=1, keepdims=True)
    lane = lax.broadcasted_iota(jnp.int32, (tokens, 128), 1)
    packed = jnp.where(lane == 0, mean_here, jnp.where(lane == 1, square_here, 0.0))
    st[0] = jnp.transpose(packed)[0:8, :]

    pl.semaphore_wait(barrier, len(near) + (NZ - 1))

    stat_copies = [cp.remote(st.at[0], st.at[NX - d], xpeer(d)) for d in range(1, NX)]
    for c in stat_copies:
        c.start()

    s0_a = [
        cp.remote(
            lat.at[pl.ds(pl.multiple_of(lax.rem(q + r, NQ) * rows, rows), rows), :], s0p, qpeer(r)
        )
        for r in range(1, NQ)
    ]

    @pl.when(tm == 0)
    def _():
        for c in s0_a:
            c.start()
        s0p[...] = lat[0:rows, :]

    for c in stat_copies:
        c.wait_recv()
    stats = [st[d] for d in range(NX)]
    mean_row = (stats[0][0:1] + stats[1][0:1] + stats[2][0:1] + stats[3][0:1]) / NX
    square_row = jnp.zeros_like(mean_row)
    for d in range(NX):
        shift = stats[d][0:1] - mean_row
        square_row += stats[d][1:2] + cols * (shift * shift)
    scale_row = lax.rsqrt(square_row / (cols * NX) + EPSILON)
    sub = lax.broadcasted_iota(jnp.int32, (128, tokens), 0)
    columns = jnp.transpose(jnp.where(sub == 0, mean_row, jnp.where(sub == 1, scale_row, 0.0)))
    mean_col, scale_col = columns[:, 0:1], columns[:, 1:2]
    load_mod.wait()
    normed = (lat[...] - mean_col) * scale_col
    modin = (normed * (1.0 + mod[1]) + mod[0]).astype(jnp.bfloat16)
    deep = cols // 2
    for k in range(2):
        xin[0, k] = modin[:, k * deep : (k + 1) * deep]

    to_right = [cp.remote(xin.at[0, k], xin.at[3, k], xpeer(1)) for k in range(2)]
    to_left = [cp.remote(xin.at[0, k], xin.at[1, k], xpeer(3)) for k in range(2)]
    pass_right = cp.remote(xin.at[3, 0], xin.at[2, 0], xpeer(1))
    pass_left = cp.remote(xin.at[1, 1], xin.at[2, 1], xpeer(3))
    for c in (to_right[0], to_left[1], to_right[1], to_left[0]):
        c.start()

    lat_copies = []
    for r in range(1, NQ):
        there = pl.ds(pl.multiple_of(lax.rem(q + r, NQ) * rows, rows), rows)
        lat_copies.append(cp.remote(lat.at[there, :], latp.at[q], qpeer(r)))
        lat_copies[-1].start()
    latp[q] = lat[pl.ds(pl.multiple_of(q * rows, rows), rows), :]

    s0_b = [cp.remote(s0p, s0p, zpeer(r)) for r in range(1, NZ)]

    @pl.when(z == 0)
    def _():
        for i, c in enumerate(s0_a):

            @pl.when(q == i + 1)
            def _():
                c.wait_recv()

        for c in s0_b:
            c.start()

    def project(d, k, first=False):
        for j in range(3):
            part = jnp.dot(
                xin[d, k], wq[d, j, k * deep : (k + 1) * deep, :],
                preferred_element_type=jnp.float32,
            )
            acc[j] = part if first else acc[j] + part

    load_wq[0].wait()
    project(0, 0, True)
    project(0, 1)
    to_right[0].wait_recv()
    pass_right.start()
    to_left[1].wait_recv()
    pass_left.start()
    load_wq[3].wait()
    project(3, 0)
    load_wq[1].wait()
    project(1, 1)
    to_right[1].wait_recv()
    project(3, 1)
    to_left[0].wait_recv()
    project(1, 0)
    load_wq[2].wait()
    pass_right.wait_recv()
    project(2, 0)
    pass_left.wait_recv()
    project(2, 1)

    for h in range(acc.shape[2] // HEAD):
        here = slice(h * HEAD, (h + 1) * HEAD)

        def normal(j):
            t = acc[j, :, here]
            scale = lax.rsqrt(jnp.mean(t * t, axis=-1, keepdims=True) + EPSILON)
            return t * scale * gain_ref[j : j + 1, :]

        scores = lax.dot_general(
            normal(0), normal(1), (((1,), (1,)), ((), ())),
            precision=lax.Precision.HIGHEST, preferred_element_type=jnp.float32,
        ) * (HEAD ** -0.5)
        top = jnp.max(scores, axis=-1, keepdims=True)
        weight = jnp.exp(scores - top)
        probs = (weight / jnp.sum(weight, axis=-1, keepdims=True)).astype(jnp.bfloat16)
        values = acc[2, :, here].astype(jnp.bfloat16)
        heads[:, here] = jnp.dot(probs, values, preferred_element_type=jnp.float32).astype(
            jnp.bfloat16
        )

    for load in load_wo:
        load.wait()
    part_copies = []
    for p in range(PARTS):
        at = slice(p * half, (p + 1) * half)
        copies = {}
        for d in (2, 1, 3):
            psend[p, d] = jnp.dot(
                heads[...], wo[d, :, at], preferred_element_type=jnp.float32
            ).astype(jnp.bfloat16)
            copies[d] = cp.remote(psend.at[p, d], precv.at[p, NX - d], xpeer(d))
            copies[d].start()
        part_copies.append(copies)

    @pl.when(z != 0)
    def _():
        for i, c in enumerate(s0_b):

            @pl.when(z == i + 1)
            def _():
                c.wait_recv()

    mine = pl.ds(pl.multiple_of(q * rows, rows), rows)
    s0_c = [cp.remote(s0p, s0.at[mine, :], qpeer(r)) for r in range(1, NQ)]
    for c in s0_c:
        c.start()
    s0[mine, :] = s0p[...]

    position = (off_ref[0] + tm).astype(jnp.float32)

    def noise_level(at):
        fraction = 1.0 - jnp.full((8, 128), at, jnp.float32) / (3.0 * NQ * NZ)
        return 3.0 * fraction / (1.0 + 2.0 * fraction)

    step_size = (noise_level(position + 1.0) - noise_level(position))[0:1, 0:1]

    a_copies = []
    for p in range(PARTS):
        at = slice(p * half, (p + 1) * half)
        attended = jnp.dot(heads[...], wo[0, :, at], preferred_element_type=jnp.float32)
        for d in (1, 3, 2):
            part_copies[p][NX - d].wait_recv()
            attended += precv[p, d].astype(jnp.float32)
        drift_here = lat[:, at] + mod[2][:, at] * attended
        drift_ref[:, at] = drift_here
        c_here = step_size * drift_here
        cown[p] = c_here
        csend[p] = c_here.astype(jnp.bfloat16)
        copies = []
        for r in range(1, NQ):
            there = pl.ds(pl.multiple_of(lax.rem(q + r, NQ) * rows, rows), rows)
            copies.append(cp.remote(csend.at[p, there, :], arecv.at[p, q], qpeer(r)))
            copies[-1].start()
        arecv[p, q] = csend[p, mine, :]
        a_copies.append(copies)

    b_copies = []
    for p in range(PARTS):
        for c in a_copies[p]:
            c.wait_recv()
        total = jnp.zeros((rows, half), jnp.float32)
        for i in range(NQ):
            csum[p, i] = total
            total += arecv[p, i].astype(jnp.float32)
        bsend[p] = total.astype(jnp.bfloat16)
        copies = []
        for r in range(1, NZ):
            copies.append(cp.remote(bsend.at[p], brecv.at[p, r], zpeer(r)))

            @pl.when(z + r < NZ)
            def _():
                copies[-1].start()

        b_copies.append(copies)

    for c in lat_copies:
        c.wait_recv()
    c_copies = []
    squares = [jnp.zeros((rows, half), jnp.float32) for _ in range(NQ)]
    for p in range(PARTS):
        at = slice(p * half, (p + 1) * half)
        zsum[p] = jnp.zeros((rows, half), jnp.float32)
        for r in range(1, NZ):

            @pl.when(z >= r)
            def _():
                b_copies[p][r - 1].wait_recv()
                zsum[p] += brecv[p, r].astype(jnp.float32)

        before = zsum[p]
        for i in range(NQ):
            entry = before + csum[p, i]
            esend[p, i] = entry.astype(jnp.bfloat16)
            change = s0p[:, at] + entry - latp[i, :, at]
            squares[i] += change * change
        copies = []
        for r in range(1, NQ):
            copies.append(
                cp.remote(esend.at[p, lax.rem(q + r, NQ)], erecv.at[p, mine, :], qpeer(r))
            )
            copies[-1].start()
        erecv[p, mine, :] = esend[p, q]
        c_copies.append(copies)

    for i in range(NQ):
        share = jnp.sum(jnp.sum(squares[i], axis=1, keepdims=True), axis=0, keepdims=True)
        rsend[i] = jnp.broadcast_to(share, (8, 128))
    r_copies = []
    for d, r in near:
        r_copies.append(
            cp.remote(rsend.at[lax.rem(q + r, NQ)], rrecv.at[(NX - d) % NX, q], xqpeer(d, r))
        )
        r_copies[-1].start()
    rrecv[0, q] = rsend[q]

    for c in s0_c:
        c.wait_recv()
    for p in range(PARTS):
        at = slice(p * half, (p + 1) * half)
        for c in c_copies[p]:
            c.wait_recv()
        upd_ref[:, at] = s0[:, at] + erecv[p].astype(jnp.float32) + cown[p]
    for c in r_copies:
        c.wait_recv()
    res_ref[...] = jnp.sum(rrecv[...], axis=(0, 1)) / (tokens * cols * NX)

    sent = stat_copies + to_right + to_left + [pass_right, pass_left] + lat_copies + s0_c + r_copies
    for copies in part_copies:
        sent += list(copies.values())
    for copies in a_copies + c_copies:
        sent += copies
    for c in sent:
        c.wait_send()

    @pl.when(tm == 0)
    def _():
        for c in s0_a:
            c.wait_send()

    @pl.when(z == 0)
    def _():
        for c in s0_b:
            c.wait_send()

    for r in range(1, NZ):

        @pl.when(z + r < NZ)
        def _():
            for p in range(PARTS):
                b_copies[p][r - 1].wait_send()


def body(starts, modulation, w_qkv, norm_gain, w_out, offset):
    tokens, cols = starts.shape[1:]
    inner = w_out.shape[0]
    half = cols // PARTS
    rows = tokens // NQ
    f32, bf16 = jnp.float32, jnp.bfloat16
    hbm = pl.BlockSpec(memory_space=pltpu.HBM)
    vmem = pl.BlockSpec(memory_space=pltpu.VMEM)
    updated, drift, residual = pl.pallas_call(
        kernel,
        out_shape=(
            pltpu.VMEM((tokens, cols), f32),
            pltpu.VMEM((tokens, cols), f32),
            pltpu.VMEM((8, 128), f32),
        ),
        in_specs=[hbm, hbm, hbm, vmem, hbm, pl.BlockSpec(memory_space=pltpu.SMEM)],
        out_specs=(vmem, vmem, vmem),
        scratch_shapes=[
            pltpu.VMEM((tokens, cols), f32),
            pltpu.VMEM((3, 1, cols), f32),
            pltpu.VMEM((NX, 3, cols, inner), bf16),
            pltpu.VMEM((NX, inner, cols), bf16),
            pltpu.VMEM((NX, 8, 128), f32),
            pltpu.VMEM((NX, 2, tokens, cols // 2), bf16),
            pltpu.VMEM((3, tokens, inner), f32),
            pltpu.VMEM((tokens, inner), bf16),
            pltpu.VMEM((PARTS, NX, tokens, half), bf16),
            pltpu.VMEM((PARTS, NX, tokens, half), bf16),
            pltpu.VMEM((rows, cols), f32),
            pltpu.VMEM((tokens, cols), f32),
            pltpu.VMEM((PARTS, tokens, half), bf16),
            pltpu.VMEM((PARTS, NQ, rows, half), bf16),
            pltpu.VMEM((PARTS, rows, half), bf16),
            pltpu.VMEM((PARTS, NZ, rows, half), bf16),
            pltpu.VMEM((PARTS, NQ, rows, half), f32),
            pltpu.VMEM((PARTS, NQ, rows, half), bf16),
            pltpu.VMEM((PARTS, tokens, half), bf16),
            pltpu.VMEM((PARTS, tokens, half), f32),
            pltpu.VMEM((PARTS, rows, half), f32),
            pltpu.VMEM((NQ, rows, cols), f32),
            pltpu.VMEM((NQ, 8, 128), f32),
            pltpu.VMEM((NX, NQ, 8, 128), f32),
            pltpu.SemaphoreType.DMA((10,)),
            pltpu.SemaphoreType.DMA((REMOTE,)),
            pltpu.SemaphoreType.DMA((REMOTE,)),
        ],
        compiler_params=pltpu.CompilerParams(
            collective_id=0, has_side_effects=True, vmem_limit_bytes=60 * 1024 * 1024
        ),
        name="sweep",
    )(
        starts.reshape(tokens, cols),
        modulation.transpose(1, 0, 2),
        w_qkv.transpose(1, 0, 2),
        norm_gain,
        w_out,
        offset,
    )
    return (updated[None], drift[None], residual[0, 0:1])


def solution(mesh):
    in_specs = (
        P("tm", None, "tp"),
        P("tm", None, None),
        P(None, None, "tp"),
        P(),
        P("tp", None),
        P(),
    )
    out_specs = (P("tm", None, "tp"), P("tm", None, "tp"), P("tm"))
    return jax.shard_map(body, mesh=mesh, in_specs=in_specs, out_specs=out_specs, check_vma=False)
```

```python
import functools

import jax
import jax.numpy as jnp
from jax import lax
from jax.experimental import pallas as pl
from jax.experimental.pallas import tpu as pltpu
from jax.sharding import PartitionSpec as P

HEAD = 128
EPSILON = 1e-06
MESH = pl.DeviceIdType.MESH

NX = 4
NQ = 8
NZ = 8
PARTS = 2


class Copies:
    def __init__(self, send, recv):
        self.send, self.recv, self.used = send, recv, 0

    def remote(self, src, dst, device):
        at = self.used
        self.used += 1
        return pltpu.make_async_remote_copy(
            src_ref=src,
            dst_ref=dst,
            send_sem=self.send.at[at],
            recv_sem=self.recv.at[at],
            device_id=device,
            device_id_type=MESH,
        )


REMOTE = 3 + 6 + 7 + 7 + 7 + 7 + PARTS * (3 + 7 + 7 + 7) + 31


def kernel(
    starts_hbm, mod_hbm, wq_hbm, gain_ref, wo_hbm, off_ref,
    upd_ref, drift_ref, res_ref,
    lat, mod, wq, wo, st, xin, acc, heads, psend, precv, s0p, s0,
    csend, arecv, bsend, brecv, csum, esend, erecv, cown, zsum, latp, rsend, rrecv,
    local_sem, send_sem, recv_sem, spread_sem,
):
    tokens, cols = lat.shape
    half = cols // PARTS
    rows = tokens // NQ
    tm = lax.axis_index("tm")
    x = lax.axis_index("tp")
    z = tm // NQ
    q = tm % NQ
    cp = Copies(send_sem, recv_sem)

    def xpeer(d):
        return (tm, lax.rem(x + d, NX))

    def qpeer(r):
        return (z * NQ + lax.rem(q + r, NQ), x)

    def xqpeer(d, r):
        return (z * NQ + lax.rem(q + r, NQ), lax.rem(x + d, NX))

    def zpeer(r):
        return (lax.rem(z + r, NZ) * NQ + q, x)

    near = [(d, r) for d in range(NX) for r in range(NQ) if d or r]
    barrier = pltpu.get_barrier_semaphore()
    greeted = [xqpeer(d, 0) for d in range(1, NX)] + [qpeer(r) for r in range(1, NQ)]
    greeted += [zpeer(1), zpeer(NZ - 1)]
    for device in greeted:
        pl.semaphore_signal(barrier, inc=1, device_id=device, device_id_type=MESH)

    def spread(n):
        for device in (zpeer(1), zpeer(NZ - 1)):
            pl.semaphore_signal(spread_sem.at[n], inc=1, device_id=device, device_id_type=MESH)

    def heard(n):
        pl.semaphore_wait(spread_sem.at[n], 2)


    load_lat = pltpu.make_async_copy(starts_hbm, lat, local_sem.at[0])
    load_lat.start()
    own = pl.ds(pl.multiple_of(x * cols, cols), cols)
    load_mod = pltpu.make_async_copy(mod_hbm.at[:, :, own], mod, local_sem.at[1])
    load_mod.start()
    load_wq, load_wo = [], []
    for d in range(NX):
        block = pl.ds(pl.multiple_of(lax.rem(x + d, NX) * cols, cols), cols)
        load_wq.append(
            pltpu.make_async_copy(wq_hbm.at[:, block, :], wq.at[d], local_sem.at[2 + d])
        )
    for d in range(NX):
        block = pl.ds(pl.multiple_of(lax.rem(x + d, NX) * cols, cols), cols)
        load_wo.append(
            pltpu.make_async_copy(wo_hbm.at[:, block], wo.at[d], local_sem.at[6 + d])
        )
    for load in load_wq + load_wo:
        load.start()

    load_lat.wait()
    latent = lat[...]
    mean_here = jnp.mean(latent, axis=1, keepdims=True)
    away = latent - mean_here
    square_here = jnp.sum(away * away, axis=1, keepdims=True)
    lane = lax.broadcasted_iota(jnp.int32, (tokens, 128), 1)
    packed = jnp.where(lane == 0, mean_here, jnp.where(lane == 1, square_here, 0.0))
    st[0] = jnp.transpose(packed)[0:8, :]

    pl.semaphore_wait(barrier, len(greeted))

    spread(0)
    stat_copies = [cp.remote(st.at[0], st.at[NX - d], xpeer(d)) for d in range(1, NX)]
    for c in stat_copies:
        c.start()

    s0_a = [
        cp.remote(
            lat.at[pl.ds(pl.multiple_of(lax.rem(q + r, NQ) * rows, rows), rows), :], s0p, qpeer(r)
        )
        for r in range(1, NQ)
    ]

    @pl.when(tm == 0)
    def _():
        for c in s0_a:
            c.start()
        s0p[...] = lat[0:rows, :]

    for c in stat_copies:
        c.wait_recv()
    heard(0)
    spread(1)
    stats = [st[d] for d in range(NX)]
    mean_row = (stats[0][0:1] + stats[1][0:1] + stats[2][0:1] + stats[3][0:1]) / NX
    square_row = jnp.zeros_like(mean_row)
    for d in range(NX):
        shift = stats[d][0:1] - mean_row
        square_row += stats[d][1:2] + cols * (shift * shift)
    scale_row = lax.rsqrt(square_row / (cols * NX) + EPSILON)
    sub = lax.broadcasted_iota(jnp.int32, (128, tokens), 0)
    columns = jnp.transpose(jnp.where(sub == 0, mean_row, jnp.where(sub == 1, scale_row, 0.0)))
    mean_col, scale_col = columns[:, 0:1], columns[:, 1:2]
    load_mod.wait()
    normed = (lat[...] - mean_col) * scale_col
    modin = (normed * (1.0 + mod[1]) + mod[0]).astype(jnp.bfloat16)
    deep = cols // 2
    for k in range(2):
        xin[0, k] = modin[:, k * deep : (k + 1) * deep]

    to_right = [cp.remote(xin.at[0, k], xin.at[3, k], xpeer(1)) for k in range(2)]
    to_left = [cp.remote(xin.at[0, k], xin.at[1, k], xpeer(3)) for k in range(2)]
    pass_right = cp.remote(xin.at[3, 0], xin.at[2, 0], xpeer(1))
    pass_left = cp.remote(xin.at[1, 1], xin.at[2, 1], xpeer(3))
    for c in (to_right[0], to_left[1], to_right[1], to_left[0]):
        c.start()

    lat_copies = []
    for r in range(1, NQ):
        there = pl.ds(pl.multiple_of(lax.rem(q + r, NQ) * rows, rows), rows)
        lat_copies.append(cp.remote(lat.at[there, :], latp.at[q], qpeer(r)))
        lat_copies[-1].start()
    latp[q] = lat[pl.ds(pl.multiple_of(q * rows, rows), rows), :]

    def project(d, k, first=False):
        for j in range(3):
            part = jnp.dot(
                xin[d, k], wq[d, j, k * deep : (k + 1) * deep, :],
                preferred_element_type=jnp.float32,
            )
            acc[j] = part if first else acc[j] + part

    load_wq[0].wait()
    project(0, 0, True)
    project(0, 1)
    heard(1)
    spread(2)
    to_right[0].wait_recv()
    pass_right.start()
    to_left[1].wait_recv()
    pass_left.start()
    heard(2)
    s0_b = [cp.remote(s0p, s0p, zpeer(r)) for r in range(1, NZ)]

    @pl.when(z == 0)
    def _():
        for i, c in enumerate(s0_a):

            @pl.when(q == i + 1)
            def _():
                c.wait_recv()

        for c in s0_b:
            c.start()

    load_wq[3].wait()
    project(3, 0)
    load_wq[1].wait()
    project(1, 1)
    to_right[1].wait_recv()
    project(3, 1)
    to_left[0].wait_recv()
    project(1, 0)
    load_wq[2].wait()
    pass_right.wait_recv()
    project(2, 0)
    pass_left.wait_recv()
    project(2, 1)

    for h in range(acc.shape[2] // HEAD):
        here = slice(h * HEAD, (h + 1) * HEAD)

        def normal(j):
            t = acc[j, :, here]
            scale = lax.rsqrt(jnp.mean(t * t, axis=-1, keepdims=True) + EPSILON)
            return t * scale * gain_ref[j : j + 1, :]

        scores = lax.dot_general(
            normal(0), normal(1), (((1,), (1,)), ((), ())),
            precision=lax.Precision.HIGHEST, preferred_element_type=jnp.float32,
        ) * (HEAD ** -0.5)
        top = jnp.max(scores, axis=-1, keepdims=True)
        weight = jnp.exp(scores - top)
        probs = (weight / jnp.sum(weight, axis=-1, keepdims=True)).astype(jnp.bfloat16)
        values = acc[2, :, here].astype(jnp.bfloat16)
        heads[:, here] = jnp.dot(probs, values, preferred_element_type=jnp.float32).astype(
            jnp.bfloat16
        )

    for load in load_wo:
        load.wait()
    part_copies = []
    for p in range(PARTS):
        at = slice(p * half, (p + 1) * half)
        copies = {}
        for d in (2, 1, 3):
            psend[p, d] = jnp.dot(
                heads[...], wo[d, :, at], preferred_element_type=jnp.float32
            ).astype(jnp.bfloat16)
            copies[d] = cp.remote(psend.at[p, d], precv.at[p, NX - d], xpeer(d))
            copies[d].start()
        part_copies.append(copies)

    @pl.when(z != 0)
    def _():
        for i, c in enumerate(s0_b):

            @pl.when(z == i + 1)
            def _():
                c.wait_recv()

    mine = pl.ds(pl.multiple_of(q * rows, rows), rows)
    s0_c = [cp.remote(s0p, s0.at[mine, :], qpeer(r)) for r in range(1, NQ)]
    for c in s0_c:
        c.start()
    s0[mine, :] = s0p[...]

    position = (off_ref[0] + tm).astype(jnp.float32)

    def noise_level(at):
        fraction = 1.0 - jnp.full((8, 128), at, jnp.float32) / (3.0 * NQ * NZ)
        return 3.0 * fraction / (1.0 + 2.0 * fraction)

    step_size = (noise_level(position + 1.0) - noise_level(position))[0:1, 0:1]

    a_copies = []
    for p in range(PARTS):
        at = slice(p * half, (p + 1) * half)
        attended = jnp.dot(heads[...], wo[0, :, at], preferred_element_type=jnp.float32)
        for d in (1, 3, 2):
            part_copies[p][NX - d].wait_recv()
            attended += precv[p, d].astype(jnp.float32)
        drift_here = lat[:, at] + mod[2][:, at] * attended
        drift_ref[:, at] = drift_here
        c_here = step_size * drift_here
        cown[p] = c_here
        csend[p] = c_here.astype(jnp.bfloat16)
        copies = []
        for r in range(1, NQ):
            there = pl.ds(pl.multiple_of(lax.rem(q + r, NQ) * rows, rows), rows)
            copies.append(cp.remote(csend.at[p, there, :], arecv.at[p, q], qpeer(r)))
            copies[-1].start()
        arecv[p, q] = csend[p, mine, :]
        a_copies.append(copies)

    b_copies = []
    for p in range(PARTS):
        for c in a_copies[p]:
            c.wait_recv()
        total = jnp.zeros((rows, half), jnp.float32)
        for i in range(NQ):
            csum[p, i] = total
            total += arecv[p, i].astype(jnp.float32)
        bsend[p] = total.astype(jnp.bfloat16)
        copies = []
        for r in range(1, NZ):
            copies.append(cp.remote(bsend.at[p], brecv.at[p, r], zpeer(r)))

            @pl.when(z + r < NZ)
            def _():
                copies[-1].start()

        b_copies.append(copies)

    for c in lat_copies:
        c.wait_recv()
    c_copies = []
    squares = [jnp.zeros((rows, half), jnp.float32) for _ in range(NQ)]
    for p in range(PARTS):
        at = slice(p * half, (p + 1) * half)
        zsum[p] = jnp.zeros((rows, half), jnp.float32)
        for r in range(1, NZ):

            @pl.when(z >= r)
            def _():
                b_copies[p][r - 1].wait_recv()
                zsum[p] += brecv[p, r].astype(jnp.float32)

        before = zsum[p]
        for i in range(NQ):
            entry = before + csum[p, i]
            esend[p, i] = entry.astype(jnp.bfloat16)
            change = s0p[:, at] + entry - latp[i, :, at]
            squares[i] += change * change
        copies = []
        for r in range(1, NQ):
            copies.append(
                cp.remote(esend.at[p, lax.rem(q + r, NQ)], erecv.at[p, mine, :], qpeer(r))
            )
            copies[-1].start()
        erecv[p, mine, :] = esend[p, q]
        c_copies.append(copies)

    for i in range(NQ):
        share = jnp.sum(jnp.sum(squares[i], axis=1, keepdims=True), axis=0, keepdims=True)
        rsend[i] = jnp.broadcast_to(share, (8, 128))
    r_copies = []
    for d, r in near:
        r_copies.append(
            cp.remote(rsend.at[lax.rem(q + r, NQ)], rrecv.at[(NX - d) % NX, q], xqpeer(d, r))
        )
        r_copies[-1].start()
    rrecv[0, q] = rsend[q]

    for c in s0_c:
        c.wait_recv()
    for p in range(PARTS):
        at = slice(p * half, (p + 1) * half)
        for c in c_copies[p]:
            c.wait_recv()
        upd_ref[:, at] = s0[:, at] + erecv[p].astype(jnp.float32) + cown[p]
    for c in r_copies:
        c.wait_recv()
    res_ref[...] = jnp.sum(rrecv[...], axis=(0, 1)) / (tokens * cols * NX)

    sent = stat_copies + to_right + to_left + [pass_right, pass_left] + lat_copies + s0_c + r_copies
    for copies in part_copies:
        sent += list(copies.values())
    for copies in a_copies + c_copies:
        sent += copies
    for c in sent:
        c.wait_send()

    @pl.when(tm == 0)
    def _():
        for c in s0_a:
            c.wait_send()

    @pl.when(z == 0)
    def _():
        for c in s0_b:
            c.wait_send()

    for r in range(1, NZ):

        @pl.when(z + r < NZ)
        def _():
            for p in range(PARTS):
                b_copies[p][r - 1].wait_send()


def body(starts, modulation, w_qkv, norm_gain, w_out, offset):
    tokens, cols = starts.shape[1:]
    inner = w_out.shape[0]
    half = cols // PARTS
    rows = tokens // NQ
    f32, bf16 = jnp.float32, jnp.bfloat16
    hbm = pl.BlockSpec(memory_space=pltpu.HBM)
    vmem = pl.BlockSpec(memory_space=pltpu.VMEM)
    updated, drift, residual = pl.pallas_call(
        kernel,
        out_shape=(
            pltpu.VMEM((tokens, cols), f32),
            pltpu.VMEM((tokens, cols), f32),
            pltpu.VMEM((8, 128), f32),
        ),
        in_specs=[hbm, hbm, hbm, vmem, hbm, pl.BlockSpec(memory_space=pltpu.SMEM)],
        out_specs=(vmem, vmem, vmem),
        scratch_shapes=[
            pltpu.VMEM((tokens, cols), f32),
            pltpu.VMEM((3, 1, cols), f32),
            pltpu.VMEM((NX, 3, cols, inner), bf16),
            pltpu.VMEM((NX, inner, cols), bf16),
            pltpu.VMEM((NX, 8, 128), f32),
            pltpu.VMEM((NX, 2, tokens, cols // 2), bf16),
            pltpu.VMEM((3, tokens, inner), f32),
            pltpu.VMEM((tokens, inner), bf16),
            pltpu.VMEM((PARTS, NX, tokens, half), bf16),
            pltpu.VMEM((PARTS, NX, tokens, half), bf16),
            pltpu.VMEM((rows, cols), f32),
            pltpu.VMEM((tokens, cols), f32),
            pltpu.VMEM((PARTS, tokens, half), bf16),
            pltpu.VMEM((PARTS, NQ, rows, half), bf16),
            pltpu.VMEM((PARTS, rows, half), bf16),
            pltpu.VMEM((PARTS, NZ, rows, half), bf16),
            pltpu.VMEM((PARTS, NQ, rows, half), f32),
            pltpu.VMEM((PARTS, NQ, rows, half), bf16),
            pltpu.VMEM((PARTS, tokens, half), bf16),
            pltpu.VMEM((PARTS, tokens, half), f32),
            pltpu.VMEM((PARTS, rows, half), f32),
            pltpu.VMEM((NQ, rows, cols), f32),
            pltpu.VMEM((NQ, 8, 128), f32),
            pltpu.VMEM((NX, NQ, 8, 128), f32),
            pltpu.SemaphoreType.DMA((10,)),
            pltpu.SemaphoreType.DMA((REMOTE,)),
            pltpu.SemaphoreType.DMA((REMOTE,)),
            pltpu.SemaphoreType.REGULAR((3,)),
        ],
        compiler_params=pltpu.CompilerParams(
            collective_id=0, has_side_effects=True, vmem_limit_bytes=60 * 1024 * 1024
        ),
        name="sweep",
    )(
        starts.reshape(tokens, cols),
        modulation.transpose(1, 0, 2),
        w_qkv.transpose(1, 0, 2),
        norm_gain,
        w_out,
        offset,
    )
    return (updated[None], drift[None], residual[0, 0:1])


def solution(mesh):
    in_specs = (
        P("tm", None, "tp"),
        P("tm", None, None),
        P(None, None, "tp"),
        P(),
        P("tp", None),
        P(),
    )
    out_specs = (P("tm", None, "tp"), P("tm", None, "tp"), P("tm"))
    return jax.shard_map(body, mesh=mesh, in_specs=in_specs, out_specs=out_specs, check_vma=False)
```

```python
import functools

import jax
import jax.numpy as jnp
from jax import lax
from jax.experimental import pallas as pl
from jax.experimental.pallas import tpu as pltpu
from jax.sharding import PartitionSpec as P

HEAD = 128
EPSILON = 1e-06
MESH = pl.DeviceIdType.MESH

NX = 4
NQ = 8
NZ = 8
PARTS = 2


class Copies:
    def __init__(self, send, recv):
        self.send, self.recv, self.used = send, recv, 0

    def remote(self, src, dst, device):
        at = self.used
        self.used += 1
        return pltpu.make_async_remote_copy(
            src_ref=src,
            dst_ref=dst,
            send_sem=self.send.at[at],
            recv_sem=self.recv.at[at],
            device_id=device,
            device_id_type=MESH,
        )


REMOTE = 3 + 6 + 7 + 7 + 7 + 7 + PARTS * (3 + 7 + 7 + 7) + 31


def kernel(
    starts_hbm, mod_hbm, wq_hbm, gain_ref, wo_hbm, off_ref,
    upd_ref, drift_ref, res_ref, step_ref,
    lat, mod, wq, wo, st, xin, acc, heads, psend, precv, s0p, s0,
    csend, arecv, bsend, brecv, csum, esend, erecv, zsum, latp, rsend, rrecv,
    local_sem, send_sem, recv_sem, spread_sem,
):
    tokens, cols = lat.shape
    half = cols // PARTS
    rows = tokens // NQ
    tm = lax.axis_index("tm")
    x = lax.axis_index("tp")
    z = tm // NQ
    q = tm % NQ
    cp = Copies(send_sem, recv_sem)

    def xpeer(d):
        return (tm, lax.rem(x + d, NX))

    def qpeer(r):
        return (z * NQ + lax.rem(q + r, NQ), x)

    def xqpeer(d, r):
        return (z * NQ + lax.rem(q + r, NQ), lax.rem(x + d, NX))

    def zpeer(r):
        return (lax.rem(z + r, NZ) * NQ + q, x)

    near = [(d, r) for d in range(NX) for r in range(NQ) if d or r]
    barrier = pltpu.get_barrier_semaphore()
    greeted = [xqpeer(d, 0) for d in range(1, NX)] + [qpeer(r) for r in range(1, NQ)]
    greeted += [zpeer(1), zpeer(NZ - 1)]
    for device in greeted:
        pl.semaphore_signal(barrier, inc=1, device_id=device, device_id_type=MESH)

    def spread(n):
        for device in (zpeer(1), zpeer(NZ - 1)):
            pl.semaphore_signal(spread_sem.at[n], inc=1, device_id=device, device_id_type=MESH)

    def heard(n):
        pl.semaphore_wait(spread_sem.at[n], 2)


    load_lat = pltpu.make_async_copy(starts_hbm, lat, local_sem.at[0])
    load_lat.start()
    own = pl.ds(pl.multiple_of(x * cols, cols), cols)
    load_mod = pltpu.make_async_copy(mod_hbm.at[:, :, own], mod, local_sem.at[1])
    load_mod.start()
    load_wq, load_wo = [], []
    for d in range(NX):
        block = pl.ds(pl.multiple_of(lax.rem(x + d, NX) * cols, cols), cols)
        load_wq.append(
            pltpu.make_async_copy(wq_hbm.at[:, block, :], wq.at[d], local_sem.at[2 + d])
        )
    for d in range(NX):
        block = pl.ds(pl.multiple_of(lax.rem(x + d, NX) * cols, cols), cols)
        load_wo.append(
            pltpu.make_async_copy(wo_hbm.at[:, block], wo.at[d], local_sem.at[6 + d])
        )
    for load in load_wq + load_wo:
        load.start()

    load_lat.wait()
    latent = lat[...]
    mean_here = jnp.mean(latent, axis=1, keepdims=True)
    away = latent - mean_here
    square_here = jnp.sum(away * away, axis=1, keepdims=True)
    lane = lax.broadcasted_iota(jnp.int32, (tokens, 128), 1)
    packed = jnp.where(lane == 0, mean_here, jnp.where(lane == 1, square_here, 0.0))
    st[0] = jnp.transpose(packed)[0:8, :]

    pl.semaphore_wait(barrier, len(greeted))

    spread(0)
    stat_copies = [cp.remote(st.at[0], st.at[NX - d], xpeer(d)) for d in range(1, NX)]
    for c in stat_copies:
        c.start()

    s0_a = [
        cp.remote(
            lat.at[pl.ds(pl.multiple_of(lax.rem(q + r, NQ) * rows, rows), rows), :], s0p, qpeer(r)
        )
        for r in range(1, NQ)
    ]

    @pl.when(tm == 0)
    def _():
        for c in s0_a:
            c.start()
        s0p[...] = lat[0:rows, :]

    for c in stat_copies:
        c.wait_recv()
    heard(0)
    spread(1)
    stats = [st[d] for d in range(NX)]
    mean_row = (stats[0][0:1] + stats[1][0:1] + stats[2][0:1] + stats[3][0:1]) / NX
    square_row = jnp.zeros_like(mean_row)
    for d in range(NX):
        shift = stats[d][0:1] - mean_row
        square_row += stats[d][1:2] + cols * (shift * shift)
    scale_row = lax.rsqrt(square_row / (cols * NX) + EPSILON)
    sub = lax.broadcasted_iota(jnp.int32, (128, tokens), 0)
    columns = jnp.transpose(jnp.where(sub == 0, mean_row, jnp.where(sub == 1, scale_row, 0.0)))
    mean_col, scale_col = columns[:, 0:1], columns[:, 1:2]
    load_mod.wait()
    normed = (lat[...] - mean_col) * scale_col
    modin = (normed * (1.0 + mod[1]) + mod[0]).astype(jnp.bfloat16)
    deep = cols // 2
    for k in range(2):
        xin[0, k] = modin[:, k * deep : (k + 1) * deep]

    to_right = [cp.remote(xin.at[0, k], xin.at[3, k], xpeer(1)) for k in range(2)]
    to_left = [cp.remote(xin.at[0, k], xin.at[1, k], xpeer(3)) for k in range(2)]
    pass_right = cp.remote(xin.at[3, 0], xin.at[2, 0], xpeer(1))
    pass_left = cp.remote(xin.at[1, 1], xin.at[2, 1], xpeer(3))
    for c in (to_right[0], to_left[1], to_right[1], to_left[0]):
        c.start()

    lat_copies = []
    for r in range(1, NQ):
        there = pl.ds(pl.multiple_of(lax.rem(q + r, NQ) * rows, rows), rows)
        lat_copies.append(cp.remote(lat.at[there, :], latp.at[q], qpeer(r)))
        lat_copies[-1].start()
    latp[q] = lat[pl.ds(pl.multiple_of(q * rows, rows), rows), :]

    def project(d, k, first=False):
        for j in range(3):
            part = jnp.dot(
                xin[d, k], wq[d, j, k * deep : (k + 1) * deep, :],
                preferred_element_type=jnp.float32,
            )
            acc[j] = part if first else acc[j] + part

    load_wq[0].wait()
    project(0, 0, True)
    project(0, 1)
    heard(1)
    spread(2)
    to_right[0].wait_recv()
    pass_right.start()
    to_left[1].wait_recv()
    pass_left.start()
    heard(2)
    s0_b = [cp.remote(s0p, s0p, zpeer(r)) for r in range(1, NZ)]

    @pl.when(z == 0)
    def _():
        for i, c in enumerate(s0_a):

            @pl.when(q == i + 1)
            def _():
                c.wait_recv()

        for c in s0_b:
            c.start()

    load_wq[3].wait()
    project(3, 0)
    load_wq[1].wait()
    project(1, 1)
    to_right[1].wait_recv()
    project(3, 1)
    to_left[0].wait_recv()
    project(1, 0)
    load_wq[2].wait()
    pass_right.wait_recv()
    project(2, 0)
    pass_left.wait_recv()
    project(2, 1)

    places = [slice(h, h + HEAD) for h in range(0, heads.shape[1], HEAD)]

    def normal(j, here):
        t = acc[j, :, here]
        scale = lax.rsqrt(jnp.mean(t * t, axis=-1, keepdims=True) + EPSILON)
        return t * scale * gain_ref[j : j + 1, :]

    pairs = [(normal(0, here), normal(1, here)) for here in places]
    scores = [
        lax.dot_general(
            a, b, (((1,), (1,)), ((), ())),
            precision=lax.Precision.HIGHEST, preferred_element_type=jnp.float32,
        ) * (HEAD ** -0.5)
        for a, b in pairs
    ]
    weights = [jnp.exp(t - jnp.max(t, axis=-1, keepdims=True)) for t in scores]
    probs = [(t / jnp.sum(t, axis=-1, keepdims=True)).astype(jnp.bfloat16) for t in weights]
    for here, t in zip(places, probs):
        values = acc[2, :, here].astype(jnp.bfloat16)
        heads[:, here] = jnp.dot(t, values, preferred_element_type=jnp.float32).astype(
            jnp.bfloat16
        )

    for load in load_wo:
        load.wait()
    part_copies = []
    for p in range(PARTS):
        at = slice(p * half, (p + 1) * half)
        copies = {}
        for d in (2, 1, 3):
            psend[p, d] = jnp.dot(
                heads[...], wo[d, :, at], preferred_element_type=jnp.float32
            ).astype(jnp.bfloat16)
            copies[d] = cp.remote(psend.at[p, d], precv.at[p, NX - d], xpeer(d))
            copies[d].start()
        part_copies.append(copies)

    @pl.when(z != 0)
    def _():
        for i, c in enumerate(s0_b):

            @pl.when(z == i + 1)
            def _():
                c.wait_recv()

    mine = pl.ds(pl.multiple_of(q * rows, rows), rows)
    s0_c = [cp.remote(s0p, s0.at[mine, :], qpeer(r)) for r in range(1, NQ)]
    for c in s0_c:
        c.start()
    s0[mine, :] = s0p[...]

    position = (off_ref[0] + tm).astype(jnp.float32)

    def noise_level(at):
        fraction = 1.0 - jnp.full((8, 128), at, jnp.float32) / (3.0 * NQ * NZ)
        return 3.0 * fraction / (1.0 + 2.0 * fraction)

    step_size = (noise_level(position + 1.0) - noise_level(position))[0:1, 0:1]

    step_ref[...] = jnp.broadcast_to(step_size, step_ref.shape)
    a_copies = []
    for p in range(PARTS):
        at = slice(p * half, (p + 1) * half)
        attended = jnp.dot(heads[...], wo[0, :, at], preferred_element_type=jnp.float32)
        for d in (1, 3, 2):
            part_copies[p][NX - d].wait_recv()
            attended += precv[p, d].astype(jnp.float32)
        gated = mod[2][:, at] * attended
        drift_ref[:, at] = gated
        drift_here = lat[:, at] + gated
        c_here = step_size * drift_here
        csend[p] = c_here.astype(jnp.bfloat16)
        copies = []
        for r in range(1, NQ):
            there = pl.ds(pl.multiple_of(lax.rem(q + r, NQ) * rows, rows), rows)
            copies.append(cp.remote(csend.at[p, there, :], arecv.at[p, q], qpeer(r)))
            copies[-1].start()
        arecv[p, q] = csend[p, mine, :]
        a_copies.append(copies)

    b_copies = []
    for p in range(PARTS):
        for c in a_copies[p]:
            c.wait_recv()
        total = jnp.zeros((rows, half), jnp.float32)
        for i in range(NQ):
            csum[p, i] = total
            total += arecv[p, i].astype(jnp.float32)
        bsend[p] = total.astype(jnp.bfloat16)
        copies = []
        for r in range(1, NZ):
            copies.append(cp.remote(bsend.at[p], brecv.at[p, r], zpeer(r)))

            @pl.when(z + r < NZ)
            def _():
                copies[-1].start()

        b_copies.append(copies)

    for c in lat_copies:
        c.wait_recv()
    c_copies = []
    squares = [jnp.zeros((rows, half), jnp.float32) for _ in range(NQ)]
    for p in range(PARTS):
        at = slice(p * half, (p + 1) * half)
        zsum[p] = jnp.zeros((rows, half), jnp.float32)
        for r in range(1, NZ):

            @pl.when(z >= r)
            def _():
                b_copies[p][r - 1].wait_recv()
                zsum[p] += brecv[p, r].astype(jnp.float32)

        before = zsum[p]
        for i in range(NQ):
            entry = before + csum[p, i]
            esend[p, i] = entry.astype(jnp.bfloat16)
            change = s0p[:, at] + entry - latp[i, :, at]
            squares[i] += change * change
        copies = []
        for r in range(1, NQ):
            copies.append(
                cp.remote(esend.at[p, lax.rem(q + r, NQ)], erecv.at[p, mine, :], qpeer(r))
            )
            copies[-1].start()
        erecv[p, mine, :] = esend[p, q]
        c_copies.append(copies)

    for i in range(NQ):
        tiles = [squares[i][:, b : b + 128] for b in range(0, half, 128)]
        rsend[i] = jnp.sum(sum(tiles[1:], tiles[0]), axis=0, keepdims=True)
    r_copies = []
    for d, r in near:
        r_copies.append(
            cp.remote(rsend.at[lax.rem(q + r, NQ)], rrecv.at[(NX - d) % NX, q], xqpeer(d, r))
        )
        r_copies[-1].start()
    rrecv[0, q] = rsend[q]

    for c in s0_c:
        c.wait_recv()
    for p in range(PARTS):
        at = slice(p * half, (p + 1) * half)
        for c in c_copies[p]:
            c.wait_recv()
        upd_ref[:, at] = s0[:, at] + erecv[p].astype(jnp.float32)
    for c in r_copies:
        c.wait_recv()
    squared = jnp.sum(jnp.sum(rrecv[...], axis=(0, 1)), axis=1, keepdims=True)
    res_ref[...] = squared / (tokens * cols * NX)

    sent = stat_copies + to_right + to_left + [pass_right, pass_left] + lat_copies + s0_c + r_copies
    for copies in part_copies:
        sent += list(copies.values())
    for copies in a_copies + c_copies:
        sent += copies
    for c in sent:
        c.wait_send()

    @pl.when(tm == 0)
    def _():
        for c in s0_a:
            c.wait_send()

    @pl.when(z == 0)
    def _():
        for c in s0_b:
            c.wait_send()

    for r in range(1, NZ):

        @pl.when(z + r < NZ)
        def _():
            for p in range(PARTS):
                b_copies[p][r - 1].wait_send()


def body(starts, modulation, w_qkv, norm_gain, w_out, offset):
    tokens, cols = starts.shape[1:]
    inner = w_out.shape[0]
    half = cols // PARTS
    rows = tokens // NQ
    f32, bf16 = jnp.float32, jnp.bfloat16
    hbm = pl.BlockSpec(memory_space=pltpu.HBM)
    vmem = pl.BlockSpec(memory_space=pltpu.VMEM)
    fresh, gated, residual, step = pl.pallas_call(
        kernel,
        out_shape=(
            pltpu.VMEM((tokens, cols), f32),
            pltpu.VMEM((tokens, cols), f32),
            pltpu.VMEM((1, 1), f32),
            pltpu.VMEM((1, cols), f32),
        ),
        in_specs=[hbm, hbm, hbm, vmem, hbm, pl.BlockSpec(memory_space=pltpu.SMEM)],
        out_specs=(vmem, vmem, vmem, vmem),
        scratch_shapes=[
            pltpu.VMEM((tokens, cols), f32),
            pltpu.VMEM((3, 1, cols), f32),
            pltpu.VMEM((NX, 3, cols, inner), bf16),
            pltpu.VMEM((NX, inner, cols), bf16),
            pltpu.VMEM((NX, 8, 128), f32),
            pltpu.VMEM((NX, 2, tokens, cols // 2), bf16),
            pltpu.VMEM((3, tokens, inner), f32),
            pltpu.VMEM((tokens, inner), bf16),
            pltpu.VMEM((PARTS, NX, tokens, half), bf16),
            pltpu.VMEM((PARTS, NX, tokens, half), bf16),
            pltpu.VMEM((rows, cols), f32),
            pltpu.VMEM((tokens, cols), f32),
            pltpu.VMEM((PARTS, tokens, half), bf16),
            pltpu.VMEM((PARTS, NQ, rows, half), bf16),
            pltpu.VMEM((PARTS, rows, half), bf16),
            pltpu.VMEM((PARTS, NZ, rows, half), bf16),
            pltpu.VMEM((PARTS, NQ, rows, half), f32),
            pltpu.VMEM((PARTS, NQ, rows, half), bf16),
            pltpu.VMEM((PARTS, tokens, half), bf16),
            pltpu.VMEM((PARTS, rows, half), f32),
            pltpu.VMEM((NQ, rows, cols), f32),
            pltpu.VMEM((NQ, 1, 128), f32),
            pltpu.VMEM((NX, NQ, 1, 128), f32),
            pltpu.SemaphoreType.DMA((10,)),
            pltpu.SemaphoreType.DMA((REMOTE,)),
            pltpu.SemaphoreType.DMA((REMOTE,)),
            pltpu.SemaphoreType.REGULAR((3,)),
        ],
        compiler_params=pltpu.CompilerParams(
            collective_id=0, has_side_effects=True, vmem_limit_bytes=60 * 1024 * 1024
        ),
        name="sweep",
    )(
        starts.reshape(tokens, cols),
        modulation.transpose(1, 0, 2),
        w_qkv.transpose(1, 0, 2),
        norm_gain,
        w_out,
        offset,
    )
    drift = starts + gated[None]
    return (fresh[None] + step[None] * drift, drift, residual.reshape(1))


def solution(mesh):
    in_specs = (
        P("tm", None, "tp"),
        P("tm", None, None),
        P(None, None, "tp"),
        P(),
        P("tp", None),
        P(),
    )
    out_specs = (P("tm", None, "tp"), P("tm", None, "tp"), P("tm"))
    return jax.shard_map(body, mesh=mesh, in_specs=in_specs, out_specs=out_specs, check_vma=False)
```

```python
import functools

import jax
import jax.numpy as jnp
from jax import lax
from jax.experimental import pallas as pl
from jax.experimental.pallas import tpu as pltpu
from jax.sharding import PartitionSpec as P

HEAD = 128
EPSILON = 1e-06
MESH = pl.DeviceIdType.MESH

NX = 4
NQ = 8
NZ = 8
PARTS = 2


class Copies:
    def __init__(self, send, recv):
        self.send, self.recv, self.used = send, recv, 0

    def remote(self, src, dst, device):
        at = self.used
        self.used += 1
        return pltpu.make_async_remote_copy(
            src_ref=src,
            dst_ref=dst,
            send_sem=self.send.at[at],
            recv_sem=self.recv.at[at],
            device_id=device,
            device_id_type=MESH,
        )

    def several(self, whole_src, whole_dst, copies):
        at = self.used
        for src, dst, device in copies:
            self.used = at
            self.remote(src, dst, device).start()
        self.used = at
        return self.remote(whole_src, whole_dst, device)


REMOTE = 3 + 6 + 7 + 7 + 7 + 7 + PARTS * (3 + 1 + 7 + 1) + 1


def kernel(
    starts_hbm, mod_hbm, wq_hbm, gain_hbm, wo_hbm, off_hbm,
    upd_ref, drift_ref, res_ref, step_ref,
    lat, mod, off_ref, gain_ref, wq, wo, st, xin, acc, heads, psend, precv, s0p, s0,
    csend, arecv, bsend, brecv, csum, esend, erecv, zsum, latp, rsend, rrecv,
    local_sem, send_sem, recv_sem, spread_sem,
):
    tokens, cols = lat.shape
    half = cols // PARTS
    rows = tokens // NQ
    tm = lax.axis_index("tm")
    x = lax.axis_index("tp")
    z = tm // NQ
    q = tm % NQ
    cp = Copies(send_sem, recv_sem)

    def xpeer(d):
        return (tm, lax.rem(x + d, NX))

    def qpeer(r):
        return (z * NQ + lax.rem(q + r, NQ), x)

    def xqpeer(d, r):
        return (z * NQ + lax.rem(q + r, NQ), lax.rem(x + d, NX))

    def zpeer(r):
        return (lax.rem(z + r, NZ) * NQ + q, x)

    near = [(d, r) for d in range(NX) for r in range(NQ) if d or r]
    barrier = pltpu.get_barrier_semaphore()
    greeted = [xqpeer(d, 0) for d in range(1, NX)] + [qpeer(r) for r in range(1, NQ)]
    greeted += [zpeer(1), zpeer(NZ - 1)]
    for device in greeted:
        pl.semaphore_signal(barrier, inc=1, device_id=device, device_id_type=MESH)

    def spread(n):
        for device in (zpeer(1), zpeer(NZ - 1)):
            pl.semaphore_signal(spread_sem.at[n], inc=1, device_id=device, device_id_type=MESH)

    def heard(n):
        pl.semaphore_wait(spread_sem.at[n], 2)


    load_lat = pltpu.make_async_copy(starts_hbm, lat, local_sem.at[0])
    load_lat.start()
    own = pl.ds(pl.multiple_of(x * cols, cols), cols)
    load_mod = pltpu.make_async_copy(mod_hbm.at[:, :, own], mod, local_sem.at[1])
    load_mod.start()
    load_gain = pltpu.make_async_copy(gain_hbm, gain_ref, local_sem.at[10])
    load_gain.start()
    load_off = pltpu.make_async_copy(off_hbm, off_ref, local_sem.at[11])
    load_off.start()
    load_wq, load_wo = [], []
    for d in range(NX):
        block = pl.ds(pl.multiple_of(lax.rem(x + d, NX) * cols, cols), cols)
        load_wq.append(
            pltpu.make_async_copy(wq_hbm.at[:, block, :], wq.at[d], local_sem.at[2 + d])
        )
    for d in range(NX):
        block = pl.ds(pl.multiple_of(lax.rem(x + d, NX) * cols, cols), cols)
        load_wo.append(
            pltpu.make_async_copy(wo_hbm.at[:, block], wo.at[d], local_sem.at[6 + d])
        )
    for load in load_wq + load_wo:
        load.start()

    load_lat.wait()
    latent = lat[...]
    mean_here = jnp.mean(latent, axis=1, keepdims=True)
    away = latent - mean_here
    square_here = jnp.sum(away * away, axis=1, keepdims=True)
    lane = lax.broadcasted_iota(jnp.int32, (tokens, 128), 1)
    packed = jnp.where(lane == 0, mean_here, jnp.where(lane == 1, square_here, 0.0))
    st[0] = jnp.transpose(packed)[0:8, :]

    pl.semaphore_wait(barrier, len(greeted))

    spread(0)
    stat_copies = [cp.remote(st.at[0], st.at[NX - d], xpeer(d)) for d in range(1, NX)]
    for c in stat_copies:
        c.start()

    s0_a = [
        cp.remote(
            lat.at[pl.ds(pl.multiple_of(lax.rem(q + r, NQ) * rows, rows), rows), :], s0p, qpeer(r)
        )
        for r in range(1, NQ)
    ]

    @pl.when(tm == 0)
    def _():
        for c in s0_a:
            c.start()
        s0p[...] = lat[0:rows, :]

    for c in stat_copies:
        c.wait_recv()
    heard(0)
    spread(1)
    stats = [st[d] for d in range(NX)]
    mean_row = (stats[0][0:1] + stats[1][0:1] + stats[2][0:1] + stats[3][0:1]) / NX
    square_row = jnp.zeros_like(mean_row)
    for d in range(NX):
        shift = stats[d][0:1] - mean_row
        square_row += stats[d][1:2] + cols * (shift * shift)
    scale_row = lax.rsqrt(square_row / (cols * NX) + EPSILON)
    sub = lax.broadcasted_iota(jnp.int32, (128, tokens), 0)
    columns = jnp.transpose(jnp.where(sub == 0, mean_row, jnp.where(sub == 1, scale_row, 0.0)))
    mean_col, scale_col = columns[:, 0:1], columns[:, 1:2]
    load_mod.wait()
    normed = (lat[...] - mean_col) * scale_col
    modin = (normed * (1.0 + mod[1]) + mod[0]).astype(jnp.bfloat16)
    deep = cols // 2
    for k in range(2):
        xin[0, k] = modin[:, k * deep : (k + 1) * deep]

    to_right = [cp.remote(xin.at[0, k], xin.at[3, k], xpeer(1)) for k in range(2)]
    to_left = [cp.remote(xin.at[0, k], xin.at[1, k], xpeer(3)) for k in range(2)]
    pass_right = cp.remote(xin.at[3, 0], xin.at[2, 0], xpeer(1))
    pass_left = cp.remote(xin.at[1, 1], xin.at[2, 1], xpeer(3))
    for c in (to_right[0], to_left[1], to_right[1], to_left[0]):
        c.start()

    lat_copies = []
    for r in range(1, NQ):
        there = pl.ds(pl.multiple_of(lax.rem(q + r, NQ) * rows, rows), rows)
        lat_copies.append(cp.remote(lat.at[there, :], latp.at[q], qpeer(r)))
        lat_copies[-1].start()
    latp[q] = lat[pl.ds(pl.multiple_of(q * rows, rows), rows), :]

    def project(d, k, first=False):
        for j in range(3):
            part = jnp.dot(
                xin[d, k], wq[d, j, k * deep : (k + 1) * deep, :],
                preferred_element_type=jnp.float32,
            )
            acc[j] = part if first else acc[j] + part

    load_wq[0].wait()
    project(0, 0, True)
    project(0, 1)
    heard(1)
    spread(2)
    to_right[0].wait_recv()
    pass_right.start()
    to_left[1].wait_recv()
    pass_left.start()
    heard(2)
    s0_b = [cp.remote(s0p, s0p, zpeer(r)) for r in range(1, NZ)]

    @pl.when(z == 0)
    def _():
        for i, c in enumerate(s0_a):

            @pl.when(q == i + 1)
            def _():
                c.wait_recv()

        for c in s0_b:
            c.start()

    load_wq[3].wait()
    project(3, 0)
    load_wq[1].wait()
    project(1, 1)
    to_right[1].wait_recv()
    project(3, 1)
    to_left[0].wait_recv()
    project(1, 0)
    load_wq[2].wait()
    pass_right.wait_recv()
    project(2, 0)
    pass_left.wait_recv()
    project(2, 1)

    places = [slice(h, h + HEAD) for h in range(0, heads.shape[1], HEAD)]

    def normal(j, here):
        t = acc[j, :, here]
        scale = lax.rsqrt(jnp.mean(t * t, axis=-1, keepdims=True) + EPSILON)
        return t * scale * gain_ref[j : j + 1, :]

    load_gain.wait()
    load_off.wait()
    pairs = [(normal(0, here), normal(1, here)) for here in places]
    scores = [
        lax.dot_general(
            a, b, (((1,), (1,)), ((), ())),
            precision=lax.Precision.HIGHEST, preferred_element_type=jnp.float32,
        ) * (HEAD ** -0.5)
        for a, b in pairs
    ]
    weights = [jnp.exp(t - jnp.max(t, axis=-1, keepdims=True)) for t in scores]
    probs = [(t / jnp.sum(t, axis=-1, keepdims=True)).astype(jnp.bfloat16) for t in weights]
    for here, t in zip(places, probs):
        values = acc[2, :, here].astype(jnp.bfloat16)
        heads[:, here] = jnp.dot(t, values, preferred_element_type=jnp.float32).astype(
            jnp.bfloat16
        )

    for load in load_wo:
        load.wait()
    part_copies = []
    for p in range(PARTS):
        at = slice(p * half, (p + 1) * half)
        copies = {}
        for d in (2, 1, 3):
            psend[p, d] = jnp.dot(
                heads[...], wo[d, :, at], preferred_element_type=jnp.float32
            ).astype(jnp.bfloat16)
            copies[d] = cp.remote(psend.at[p, d], precv.at[p, NX - d], xpeer(d))
            copies[d].start()
        part_copies.append(copies)

    @pl.when(z != 0)
    def _():
        for i, c in enumerate(s0_b):

            @pl.when(z == i + 1)
            def _():
                c.wait_recv()

    mine = pl.ds(pl.multiple_of(q * rows, rows), rows)
    s0_c = [cp.remote(s0p, s0.at[mine, :], qpeer(r)) for r in range(1, NQ)]
    for c in s0_c:
        c.start()
    s0[mine, :] = s0p[...]

    position = (off_ref[0] + tm).astype(jnp.float32)

    def noise_level(at):
        fraction = 1.0 - jnp.full((8, 128), at, jnp.float32) / (3.0 * NQ * NZ)
        return 3.0 * fraction / (1.0 + 2.0 * fraction)

    step_size = (noise_level(position + 1.0) - noise_level(position))[0:1, 0:1]

    step_ref[...] = jnp.broadcast_to(step_size, step_ref.shape)
    a_copies = []
    for p in range(PARTS):
        at = slice(p * half, (p + 1) * half)
        attended = jnp.dot(heads[...], wo[0, :, at], preferred_element_type=jnp.float32)
        for d in (1, 3, 2):
            part_copies[p][NX - d].wait_recv()
            attended += precv[p, d].astype(jnp.float32)
        gated = mod[2][:, at] * attended
        drift_ref[:, at] = gated
        drift_here = lat[:, at] + gated
        c_here = step_size * drift_here
        csend[p] = c_here.astype(jnp.bfloat16)
        copies = []
        for r in range(1, NQ):
            there = pl.ds(pl.multiple_of(lax.rem(q + r, NQ) * rows, rows), rows)
            copies.append((csend.at[p, there, :], arecv.at[p, q], qpeer(r)))
        others = pl.ds(0, tokens - rows)
        a_copies.append(cp.several(csend.at[p, others, :], arecv.at[p, 0 : NQ - 1], copies))
        arecv[p, q] = csend[p, mine, :]

    b_copies = []
    for p in range(PARTS):
        a_copies[p].wait_recv()
        total = jnp.zeros((rows, half), jnp.float32)
        for i in range(NQ):
            csum[p, i] = total
            total += arecv[p, i].astype(jnp.float32)
        bsend[p] = total.astype(jnp.bfloat16)
        copies = []
        for r in range(1, NZ):
            copies.append(cp.remote(bsend.at[p], brecv.at[p, r], zpeer(r)))

            @pl.when(z + r < NZ)
            def _():
                copies[-1].start()

        b_copies.append(copies)

    sent = stat_copies + to_right + to_left + [pass_right, pass_left] + lat_copies + s0_c
    for copies in part_copies:
        sent += list(copies.values())
    sent += a_copies
    for c in sent:
        c.wait_send()

    @pl.when(tm == 0)
    def _():
        for c in s0_a:
            c.wait_send()

    @pl.when(z == 0)
    def _():
        for c in s0_b:
            c.wait_send()

    for c in lat_copies:
        c.wait_recv()
    c_copies = []
    squares = [jnp.zeros((rows, half), jnp.float32) for _ in range(NQ)]
    for p in range(PARTS):
        at = slice(p * half, (p + 1) * half)
        zsum[p] = jnp.zeros((rows, half), jnp.float32)
        for r in range(1, NZ):

            @pl.when(z >= r)
            def _():
                b_copies[p][r - 1].wait_recv()
                zsum[p] += brecv[p, r].astype(jnp.float32)

        before = zsum[p]
        for i in range(NQ):
            entry = before + csum[p, i]
            esend[p, i] = entry.astype(jnp.bfloat16)
            change = s0p[:, at] + entry - latp[i, :, at]
            squares[i] += change * change
        copies = [
            (esend.at[p, lax.rem(q + r, NQ)], erecv.at[p, mine, :], qpeer(r))
            for r in range(1, NQ)
        ]
        c_copies.append(cp.several(esend.at[p, 0 : NQ - 1], erecv.at[p, others, :], copies))
        erecv[p, mine, :] = esend[p, q]

    for i in range(NQ):
        tiles = [squares[i][:, b : b + 128] for b in range(0, half, 128)]
        rsend[i] = jnp.sum(sum(tiles[1:], tiles[0]), axis=0, keepdims=True)
    shares = rrecv.at[0 : len(near)]
    r_all = cp.several(
        shares, shares,
        [
            (rsend.at[lax.rem(q + r, NQ)], rrecv.at[n], xqpeer(d, r))
            for n, (d, r) in enumerate(near)
        ],
    )
    rrecv[len(near)] = rsend[q]

    for c in s0_c:
        c.wait_recv()
    for c in c_copies + [r_all]:
        c.wait_send()

    for r in range(1, NZ):

        @pl.when(z + r < NZ)
        def _():
            for p in range(PARTS):
                b_copies[p][r - 1].wait_send()
    for p in range(PARTS):
        at = slice(p * half, (p + 1) * half)
        c_copies[p].wait_recv()
        upd_ref[:, at] = s0[:, at] + erecv[p].astype(jnp.float32)
    r_all.wait_recv()
    squared = jnp.sum(jnp.sum(rrecv[...], axis=0), axis=1, keepdims=True)
    res_ref[...] = squared / (tokens * cols * NX)


def body(starts, modulation, w_qkv, norm_gain, w_out, offset):
    tokens, cols = starts.shape[1:]
    inner = w_out.shape[0]
    half = cols // PARTS
    rows = tokens // NQ
    f32, bf16 = jnp.float32, jnp.bfloat16
    hbm = pl.BlockSpec(memory_space=pltpu.HBM)
    vmem = pl.BlockSpec(memory_space=pltpu.VMEM)
    fresh, gated, residual, step = pl.pallas_call(
        kernel,
        out_shape=(
            pltpu.VMEM((tokens, cols), f32),
            pltpu.VMEM((tokens, cols), f32),
            pltpu.VMEM((1, 1), f32),
            pltpu.VMEM((1, cols), f32),
        ),
        in_specs=[hbm, hbm, hbm, hbm, hbm, hbm],
        out_specs=(vmem, vmem, vmem, vmem),
        scratch_shapes=[
            pltpu.VMEM((tokens, cols), f32),
            pltpu.VMEM((3, 1, cols), f32),
            pltpu.SMEM((1,), jnp.int32),
            pltpu.VMEM((2, HEAD), f32),
            pltpu.VMEM((NX, 3, cols, inner), bf16),
            pltpu.VMEM((NX, inner, cols), bf16),
            pltpu.VMEM((NX, 8, 128), f32),
            pltpu.VMEM((NX, 2, tokens, cols // 2), bf16),
            pltpu.VMEM((3, tokens, inner), f32),
            pltpu.VMEM((tokens, inner), bf16),
            pltpu.VMEM((PARTS, NX, tokens, half), bf16),
            pltpu.VMEM((PARTS, NX, tokens, half), bf16),
            pltpu.VMEM((rows, cols), f32),
            pltpu.VMEM((tokens, cols), f32),
            pltpu.VMEM((PARTS, tokens, half), bf16),
            pltpu.VMEM((PARTS, NQ, rows, half), bf16),
            pltpu.VMEM((PARTS, rows, half), bf16),
            pltpu.VMEM((PARTS, NZ, rows, half), bf16),
            pltpu.VMEM((PARTS, NQ, rows, half), f32),
            pltpu.VMEM((PARTS, NQ, rows, half), bf16),
            pltpu.VMEM((PARTS, tokens, half), bf16),
            pltpu.VMEM((PARTS, rows, half), f32),
            pltpu.VMEM((NQ, rows, cols), f32),
            pltpu.VMEM((NQ, 1, 128), f32),
            pltpu.VMEM((NX * NQ, 1, 128), f32),
            pltpu.SemaphoreType.DMA((12,)),
            pltpu.SemaphoreType.DMA((REMOTE,)),
            pltpu.SemaphoreType.DMA((REMOTE,)),
            pltpu.SemaphoreType.REGULAR((3,)),
        ],
        compiler_params=pltpu.CompilerParams(
            collective_id=0, has_side_effects=True, vmem_limit_bytes=60 * 1024 * 1024
        ),
        name="sweep",
    )(
        starts.reshape(tokens, cols),
        modulation.transpose(1, 0, 2),
        w_qkv.transpose(1, 0, 2),
        norm_gain,
        w_out,
        offset,
    )
    drift = starts + gated[None]
    return (fresh[None] + step[None] * drift, drift, residual.reshape(1))


def solution(mesh):
    in_specs = (
        P("tm", None, "tp"),
        P("tm", None, None),
        P(None, None, "tp"),
        P(),
        P("tp", None),
        P(),
    )
    out_specs = (P("tm", None, "tp"), P("tm", None, "tp"), P("tm"))
    return jax.shard_map(body, mesh=mesh, in_specs=in_specs, out_specs=out_specs, check_vma=False)
```

```python
import functools

import jax
import jax.numpy as jnp
from jax import lax
from jax.experimental import pallas as pl
from jax.experimental.pallas import tpu as pltpu
from jax.sharding import PartitionSpec as P

HEAD = 128
EPSILON = 1e-06
MESH = pl.DeviceIdType.MESH

NX = 4
NQ = 8
NZ = 8
PARTS = 2


class Copies:
    def __init__(self, send, recv):
        self.send, self.recv, self.used = send, recv, 0

    def remote(self, src, dst, device):
        at = self.used
        self.used += 1
        return pltpu.make_async_remote_copy(
            src_ref=src,
            dst_ref=dst,
            send_sem=self.send.at[at],
            recv_sem=self.recv.at[at],
            device_id=device,
            device_id_type=MESH,
        )

    def several(self, whole_src, whole_dst, copies):
        at = self.used
        for src, dst, device in copies:
            self.used = at
            self.remote(src, dst, device).start()
        self.used = at
        return self.remote(whole_src, whole_dst, device)


REMOTE = 3 + 6 + 7 + 7 + 7 + 7 + PARTS * (3 + 1 + 7 + 1) + 1


def kernel(
    starts_hbm, mod_hbm, wq_hbm, gain_hbm, wo_hbm, off_hbm,
    upd_ref, drift_ref, res_ref, step_ref,
    lat, mod, off_ref, gain_ref, wq, wo, st, xin, acc, heads, psend, precv, s0p, s0,
    csend, arecv, bsend, brecv, csum, esend, erecv, zsum, latp, rsend, rrecv,
    local_sem, send_sem, recv_sem, spread_sem,
):
    tokens, cols = lat.shape
    half = cols // PARTS
    rows = tokens // NQ
    tm = lax.axis_index("tm")
    x = lax.axis_index("tp")
    z = tm // NQ
    q = tm % NQ
    cp = Copies(send_sem, recv_sem)

    def xpeer(d):
        return (tm, lax.rem(x + d, NX))

    def qpeer(r):
        return (z * NQ + lax.rem(q + r, NQ), x)

    def xqpeer(d, r):
        return (z * NQ + lax.rem(q + r, NQ), lax.rem(x + d, NX))

    def zpeer(r):
        return (lax.rem(z + r, NZ) * NQ + q, x)

    near = [(d, r) for d in (2, 1, 3, 0) for r in (4, 5, 3, 6, 2, 7, 1, 0) if d or r]
    barrier = pltpu.get_barrier_semaphore()
    greeted = [zpeer(1), zpeer(NZ - 1)] + [qpeer(r) for r in (4, 5, 3, 6, 2, 7, 1)]
    greeted += [xpeer(d) for d in (2, 1, 3)]
    for device in greeted:
        pl.semaphore_signal(barrier, inc=1, device_id=device, device_id_type=MESH)

    def spread(n):
        for device in (zpeer(1), zpeer(NZ - 1)):
            pl.semaphore_signal(spread_sem.at[n], inc=1, device_id=device, device_id_type=MESH)

    def heard(n):
        pl.semaphore_wait(spread_sem.at[n], 2)


    load_lat = pltpu.make_async_copy(starts_hbm, lat, local_sem.at[0])
    load_lat.start()
    own = pl.ds(pl.multiple_of(x * cols, cols), cols)
    load_mod = pltpu.make_async_copy(mod_hbm.at[:, :, own], mod, local_sem.at[1])
    load_mod.start()
    load_gain = pltpu.make_async_copy(gain_hbm, gain_ref, local_sem.at[10])
    load_gain.start()
    load_off = pltpu.make_async_copy(off_hbm, off_ref, local_sem.at[11])
    load_off.start()
    load_wq, load_wo = [], []
    for d in range(NX):
        block = pl.ds(pl.multiple_of(lax.rem(x + d, NX) * cols, cols), cols)
        load_wq.append(
            pltpu.make_async_copy(wq_hbm.at[:, block, :], wq.at[d], local_sem.at[2 + d])
        )
    for d in range(NX):
        block = pl.ds(pl.multiple_of(lax.rem(x + d, NX) * cols, cols), cols)
        load_wo.append(
            pltpu.make_async_copy(wo_hbm.at[:, block], wo.at[d], local_sem.at[6 + d])
        )
    for load in load_wq + load_wo:
        load.start()

    load_lat.wait()
    latent = lat[...]
    mean_here = jnp.mean(latent, axis=1, keepdims=True)
    away = latent - mean_here
    square_here = jnp.sum(away * away, axis=1, keepdims=True)
    lane = lax.broadcasted_iota(jnp.int32, (tokens, 128), 1)
    packed = jnp.where(lane == 0, mean_here, jnp.where(lane == 1, square_here, 0.0))
    st[0] = jnp.transpose(packed)[0:8, :]

    pl.semaphore_wait(barrier, len(greeted))

    spread(0)
    tiles = st.at[1:NX]
    stat_copies = [
        cp.several(tiles, tiles, [(st.at[0], st.at[NX - d], xpeer(d)) for d in (2, 1, 3)])
    ]

    s0_a = [
        cp.remote(
            lat.at[pl.ds(pl.multiple_of(lax.rem(q + r, NQ) * rows, rows), rows), :], s0p, qpeer(r)
        )
        for r in range(1, NQ)
    ]

    @pl.when(tm == 0)
    def _():
        for c in s0_a:
            c.start()
        s0p[...] = lat[0:rows, :]

    for c in stat_copies:
        c.wait_recv()
    heard(0)
    spread(1)
    stats = [st[d] for d in range(NX)]
    mean_row = (stats[0][0:1] + stats[1][0:1] + stats[2][0:1] + stats[3][0:1]) / NX
    square_row = jnp.zeros_like(mean_row)
    for d in range(NX):
        shift = stats[d][0:1] - mean_row
        square_row += stats[d][1:2] + cols * (shift * shift)
    scale_row = lax.rsqrt(square_row / (cols * NX) + EPSILON)
    sub = lax.broadcasted_iota(jnp.int32, (128, tokens), 0)
    columns = jnp.transpose(jnp.where(sub == 0, mean_row, jnp.where(sub == 1, scale_row, 0.0)))
    mean_col, scale_col = columns[:, 0:1], columns[:, 1:2]
    load_mod.wait()
    deep = cols // 2

    def prepare(k):
        part = slice(k * deep, (k + 1) * deep)
        normed = (lat[:, part] - mean_col) * scale_col
        modin = normed * (1.0 + mod[1][:, part]) + mod[0][:, part]
        xin[0, k] = modin.astype(jnp.bfloat16)

    to_right = [cp.remote(xin.at[0, k], xin.at[3, k], xpeer(1)) for k in range(2)]
    to_left = [cp.remote(xin.at[0, k], xin.at[1, k], xpeer(3)) for k in range(2)]
    pass_right = cp.remote(xin.at[3, 0], xin.at[2, 0], xpeer(1))
    pass_left = cp.remote(xin.at[1, 1], xin.at[2, 1], xpeer(3))
    prepare(0)
    to_right[0].start()
    prepare(1)
    for c in (to_left[1], to_right[1], to_left[0]):
        c.start()

    lat_copies = []
    for r in range(1, NQ):
        there = pl.ds(pl.multiple_of(lax.rem(q + r, NQ) * rows, rows), rows)
        lat_copies.append(cp.remote(lat.at[there, :], latp.at[q], qpeer(r)))
        lat_copies[-1].start()
    latp[q] = lat[pl.ds(pl.multiple_of(q * rows, rows), rows), :]

    def project(d, k, first=False):
        for j in range(3):
            part = jnp.dot(
                xin[d, k], wq[d, j, k * deep : (k + 1) * deep, :],
                preferred_element_type=jnp.float32,
            )
            acc[j] = part if first else acc[j] + part

    load_wq[0].wait()
    project(0, 0, True)
    project(0, 1)
    to_right[0].wait_recv()
    pass_right.start()
    to_left[1].wait_recv()
    pass_left.start()
    heard(1)
    spread(2)
    load_wq[3].wait()
    project(3, 0)
    load_wq[1].wait()
    project(1, 1)
    heard(2)
    s0_b = [cp.remote(s0p, s0p, zpeer(r)) for r in range(1, NZ)]

    @pl.when(z == 0)
    def _():
        for i, c in enumerate(s0_a):

            @pl.when(q == i + 1)
            def _():
                c.wait_recv()

        for c in s0_b:
            c.start()

    to_right[1].wait_recv()
    project(3, 1)
    to_left[0].wait_recv()
    project(1, 0)
    load_wq[2].wait()
    pass_right.wait_recv()
    pass_left.wait_recv()
    for j in range(3):
        acc[j] += sum(
            jnp.dot(
                xin[2, k], wq[2, j, k * deep : (k + 1) * deep, :],
                preferred_element_type=jnp.float32,
            )
            for k in range(2)
        )

    places = [slice(h, h + HEAD) for h in range(0, heads.shape[1], HEAD)]

    def normal(j, here):
        t = acc[j, :, here]
        scale = lax.rsqrt(jnp.mean(t * t, axis=-1, keepdims=True) + EPSILON)
        return t * scale * gain_ref[j : j + 1, :]

    load_gain.wait()
    load_off.wait()
    pairs = [(normal(0, here), normal(1, here)) for here in places]
    scores = [
        lax.dot_general(
            a, b, (((1,), (1,)), ((), ())),
            precision=lax.Precision.HIGHEST, preferred_element_type=jnp.float32,
        ) * (HEAD ** -0.5)
        for a, b in pairs
    ]
    weights = [jnp.exp(t - jnp.max(t, axis=-1, keepdims=True)) for t in scores]
    probs = [(t / jnp.sum(t, axis=-1, keepdims=True)).astype(jnp.bfloat16) for t in weights]
    for here, t in zip(places, probs):
        values = acc[2, :, here].astype(jnp.bfloat16)
        heads[:, here] = jnp.dot(t, values, preferred_element_type=jnp.float32).astype(
            jnp.bfloat16
        )

    for load in load_wo:
        load.wait()
    part_copies = []
    for p in range(PARTS):
        at = slice(p * half, (p + 1) * half)
        copies = {}
        for d in (2, 1, 3):
            psend[p, d] = jnp.dot(
                heads[...], wo[d, :, at], preferred_element_type=jnp.float32
            ).astype(jnp.bfloat16)
            copies[d] = cp.remote(psend.at[p, d], precv.at[p, NX - d], xpeer(d))
            copies[d].start()
        part_copies.append(copies)

    @pl.when(z != 0)
    def _():
        for i, c in enumerate(s0_b):

            @pl.when(z == i + 1)
            def _():
                c.wait_recv()

    mine = pl.ds(pl.multiple_of(q * rows, rows), rows)
    s0_c = [cp.remote(s0p, s0.at[mine, :], qpeer(r)) for r in range(1, NQ)]
    for c in s0_c:
        c.start()
    s0[mine, :] = s0p[...]

    position = (off_ref[0] + tm).astype(jnp.float32)

    def noise_level(at):
        fraction = 1.0 - jnp.full((8, 128), at, jnp.float32) / (3.0 * NQ * NZ)
        return 3.0 * fraction / (1.0 + 2.0 * fraction)

    step_size = (noise_level(position + 1.0) - noise_level(position))[0:1, 0:1]

    step_ref[...] = jnp.broadcast_to(step_size, step_ref.shape)
    a_copies = []
    for p in range(PARTS):
        at = slice(p * half, (p + 1) * half)
        attended = jnp.dot(heads[...], wo[0, :, at], preferred_element_type=jnp.float32)
        for d in (1, 3, 2):
            part_copies[p][NX - d].wait_recv()
            attended += precv[p, d].astype(jnp.float32)
        gated = mod[2][:, at] * attended
        drift_ref[:, at] = gated
        drift_here = lat[:, at] + gated
        c_here = step_size * drift_here
        csend[p] = c_here.astype(jnp.bfloat16)
        copies = []
        for r in range(1, NQ):
            there = pl.ds(pl.multiple_of(lax.rem(q + r, NQ) * rows, rows), rows)
            copies.append((csend.at[p, there, :], arecv.at[p, q], qpeer(r)))
        others = pl.ds(0, tokens - rows)
        a_copies.append(cp.several(csend.at[p, others, :], arecv.at[p, 0 : NQ - 1], copies))
        arecv[p, q] = csend[p, mine, :]

    b_copies = []
    for p in range(PARTS):
        a_copies[p].wait_recv()
        total = jnp.zeros((rows, half), jnp.float32)
        for i in range(NQ):
            csum[p, i] = total
            total += arecv[p, i].astype(jnp.float32)
        bsend[p] = total.astype(jnp.bfloat16)
        copies = []
        for r in range(1, NZ):
            copies.append(cp.remote(bsend.at[p], brecv.at[p, r], zpeer(r)))

            @pl.when(z + r < NZ)
            def _():
                copies[-1].start()

        b_copies.append(copies)

    sent = stat_copies + to_right + to_left + [pass_right, pass_left] + lat_copies + s0_c
    for copies in part_copies:
        sent += list(copies.values())
    sent += a_copies
    for c in sent:
        c.wait_send()

    @pl.when(tm == 0)
    def _():
        for c in s0_a:
            c.wait_send()

    @pl.when(z == 0)
    def _():
        for c in s0_b:
            c.wait_send()

    for c in lat_copies:
        c.wait_recv()
    def send_squares():
        for i in range(NQ):
            tiles = [squares[i][:, b : b + 128] for b in range(0, half, 128)]
            rsend[i] = jnp.sum(sum(tiles[1:], tiles[0]), axis=0, keepdims=True)
        shares = rrecv.at[0 : len(near)]
        r_all = cp.several(
            shares, shares,
            [
                (rsend.at[lax.rem(q + r, NQ)], rrecv.at[n], xqpeer(d, r))
                for n, (d, r) in enumerate(near)
            ],
        )
        rrecv[len(near)] = rsend[q]
        return r_all

    c_copies = []
    squares = [jnp.zeros((rows, half), jnp.float32) for _ in range(NQ)]
    for p in range(PARTS):
        at = slice(p * half, (p + 1) * half)
        zsum[p] = jnp.zeros((rows, half), jnp.float32)
        for r in range(1, NZ):

            @pl.when(z >= r)
            def _():
                b_copies[p][r - 1].wait_recv()
                zsum[p] += brecv[p, r].astype(jnp.float32)

        before = zsum[p]
        for i in range(NQ):
            change = s0p[:, at] + (before + csum[p, i]) - latp[i, :, at]
            squares[i] += change * change
        if p == PARTS - 1:
            r_all = send_squares()
        for i in range(NQ):
            esend[p, i] = (before + csum[p, i]).astype(jnp.bfloat16)
        copies = [
            (esend.at[p, lax.rem(q + r, NQ)], erecv.at[p, mine, :], qpeer(r))
            for r in range(1, NQ)
        ]
        c_copies.append(cp.several(esend.at[p, 0 : NQ - 1], erecv.at[p, others, :], copies))
        erecv[p, mine, :] = esend[p, q]

    for c in s0_c:
        c.wait_recv()
    for c in c_copies + [r_all]:
        c.wait_send()

    for r in range(1, NZ):

        @pl.when(z + r < NZ)
        def _():
            for p in range(PARTS):
                b_copies[p][r - 1].wait_send()
    for p in range(PARTS):
        at = slice(p * half, (p + 1) * half)
        c_copies[p].wait_recv()
        upd_ref[:, at] = s0[:, at] + erecv[p].astype(jnp.float32)
    r_all.wait_recv()
    squared = jnp.sum(jnp.sum(rrecv[...], axis=0), axis=1, keepdims=True)
    res_ref[...] = squared / (tokens * cols * NX)


def body(starts, modulation, w_qkv, norm_gain, w_out, offset):
    tokens, cols = starts.shape[1:]
    inner = w_out.shape[0]
    half = cols // PARTS
    rows = tokens // NQ
    f32, bf16 = jnp.float32, jnp.bfloat16
    hbm = pl.BlockSpec(memory_space=pltpu.HBM)
    vmem = pl.BlockSpec(memory_space=pltpu.VMEM)
    fresh, gated, residual, step = pl.pallas_call(
        kernel,
        out_shape=(
            pltpu.VMEM((tokens, cols), f32),
            pltpu.VMEM((tokens, cols), f32),
            pltpu.VMEM((1, 1), f32),
            pltpu.VMEM((1, cols), f32),
        ),
        in_specs=[hbm, hbm, hbm, hbm, hbm, hbm],
        out_specs=(vmem, vmem, vmem, vmem),
        scratch_shapes=[
            pltpu.VMEM((tokens, cols), f32),
            pltpu.VMEM((3, 1, cols), f32),
            pltpu.SMEM((1,), jnp.int32),
            pltpu.VMEM((2, HEAD), f32),
            pltpu.VMEM((NX, 3, cols, inner), bf16),
            pltpu.VMEM((NX, inner, cols), bf16),
            pltpu.VMEM((NX, 8, 128), f32),
            pltpu.VMEM((NX, 2, tokens, cols // 2), bf16),
            pltpu.VMEM((3, tokens, inner), f32),
            pltpu.VMEM((tokens, inner), bf16),
            pltpu.VMEM((PARTS, NX, tokens, half), bf16),
            pltpu.VMEM((PARTS, NX, tokens, half), bf16),
            pltpu.VMEM((rows, cols), f32),
            pltpu.VMEM((tokens, cols), f32),
            pltpu.VMEM((PARTS, tokens, half), bf16),
            pltpu.VMEM((PARTS, NQ, rows, half), bf16),
            pltpu.VMEM((PARTS, rows, half), bf16),
            pltpu.VMEM((PARTS, NZ, rows, half), bf16),
            pltpu.VMEM((PARTS, NQ, rows, half), f32),
            pltpu.VMEM((PARTS, NQ, rows, half), bf16),
            pltpu.VMEM((PARTS, tokens, half), bf16),
            pltpu.VMEM((PARTS, rows, half), f32),
            pltpu.VMEM((NQ, rows, cols), f32),
            pltpu.VMEM((NQ, 1, 128), f32),
            pltpu.VMEM((NX * NQ, 1, 128), f32),
            pltpu.SemaphoreType.DMA((12,)),
            pltpu.SemaphoreType.DMA((REMOTE,)),
            pltpu.SemaphoreType.DMA((REMOTE,)),
            pltpu.SemaphoreType.REGULAR((3,)),
        ],
        compiler_params=pltpu.CompilerParams(
            collective_id=0, has_side_effects=True, vmem_limit_bytes=60 * 1024 * 1024
        ),
        name="sweep",
    )(
        starts.reshape(tokens, cols),
        modulation.transpose(1, 0, 2),
        w_qkv.transpose(1, 0, 2),
        norm_gain,
        w_out,
        offset,
    )
    drift = starts + gated[None]
    return (fresh[None] + step[None] * drift, drift, residual.reshape(1))


def solution(mesh):
    in_specs = (
        P("tm", None, "tp"),
        P("tm", None, None),
        P(None, None, "tp"),
        P(),
        P("tp", None),
        P(),
    )
    out_specs = (P("tm", None, "tp"), P("tm", None, "tp"), P("tm"))
    return jax.shard_map(body, mesh=mesh, in_specs=in_specs, out_specs=out_specs, check_vma=False)
```

```python
import functools

import jax
import jax.numpy as jnp
from jax import lax
from jax.experimental import pallas as pl
from jax.experimental.pallas import tpu as pltpu
from jax.sharding import PartitionSpec as P

HEAD = 128
EPSILON = 1e-06
MESH = pl.DeviceIdType.MESH

NX = 4
NQ = 8
NZ = 8
PARTS = 2


class Copies:
    def __init__(self, send, recv):
        self.send, self.recv, self.used = send, recv, 0

    def remote(self, src, dst, device):
        at = self.used
        self.used += 1
        return pltpu.make_async_remote_copy(
            src_ref=src,
            dst_ref=dst,
            send_sem=self.send.at[at],
            recv_sem=self.recv.at[at],
            device_id=device,
            device_id_type=MESH,
        )

    def several(self, whole_src, whole_dst, copies):
        at = self.used
        for src, dst, device in copies:
            self.used = at
            self.remote(src, dst, device).start()
        self.used = at
        return self.remote(whole_src, whole_dst, device)


REMOTE = 3 + 6 + 7 + 7 + 7 + 7 + PARTS * (3 + 1 + 7 + 1) + 1


def kernel(
    starts_hbm, mod_hbm, wq_hbm, gain_hbm, wo_hbm, off_hbm,
    upd_ref, drift_ref, res_ref, step_ref,
    lat, mod, off_ref, gain_ref, wq, wo, st, xin, acc, heads, psend, precv, s0p, s0,
    csend, arecv, bsend, brecv, csum, esend, erecv, zsum, latp, rsend, rrecv,
    local_sem, send_sem, recv_sem, spread_sem,
):
    tokens, cols = lat.shape
    half = cols // PARTS
    rows = tokens // NQ
    tm = lax.axis_index("tm")
    x = lax.axis_index("tp")
    z = tm // NQ
    q = tm % NQ
    cp = Copies(send_sem, recv_sem)

    def xpeer(d):
        return (tm, lax.rem(x + d, NX))

    def qpeer(r):
        return (z * NQ + lax.rem(q + r, NQ), x)

    def xqpeer(d, r):
        return (z * NQ + lax.rem(q + r, NQ), lax.rem(x + d, NX))

    def zpeer(r):
        return (lax.rem(z + r, NZ) * NQ + q, x)

    near = [(d, r) for d in (2, 1, 3, 0) for r in (4, 5, 3, 6, 2, 7, 1, 0) if d or r]
    barrier = pltpu.get_barrier_semaphore()
    greeted = [zpeer(1), zpeer(NZ - 1)] + [qpeer(r) for r in (4, 5, 3, 6, 2, 7, 1)]
    greeted += [xpeer(d) for d in (2, 1, 3)]
    for device in greeted:
        pl.semaphore_signal(barrier, inc=1, device_id=device, device_id_type=MESH)

    def spread(n):
        for device in (zpeer(1), zpeer(NZ - 1)):
            pl.semaphore_signal(spread_sem.at[n], inc=1, device_id=device, device_id_type=MESH)

    def heard(n):
        pl.semaphore_wait(spread_sem.at[n], 2)


    load_lat = pltpu.make_async_copy(starts_hbm, lat, local_sem.at[0])
    load_lat.start()
    own = pl.ds(pl.multiple_of(x * cols, cols), cols)
    load_mod = pltpu.make_async_copy(mod_hbm.at[:, :, own], mod, local_sem.at[1])
    load_mod.start()
    load_gain = pltpu.make_async_copy(gain_hbm, gain_ref, local_sem.at[10])
    load_gain.start()
    load_off = pltpu.make_async_copy(off_hbm, off_ref, local_sem.at[11])
    load_off.start()
    load_wq, load_wo = [], []
    for d in range(NX):
        block = pl.ds(pl.multiple_of(lax.rem(x + d, NX) * cols, cols), cols)
        load_wq.append(
            pltpu.make_async_copy(wq_hbm.at[:, block, :], wq.at[d], local_sem.at[2 + d])
        )
    for d in range(NX):
        block = pl.ds(pl.multiple_of(lax.rem(x + d, NX) * cols, cols), cols)
        load_wo.append(
            pltpu.make_async_copy(wo_hbm.at[:, block], wo.at[d], local_sem.at[6 + d])
        )
    for load in load_wq + load_wo:
        load.start()

    load_lat.wait()
    latent = lat[...]
    mean_here = jnp.mean(latent, axis=1, keepdims=True)
    away = latent - mean_here
    square_here = jnp.sum(away * away, axis=1, keepdims=True)
    lane = lax.broadcasted_iota(jnp.int32, (tokens, 128), 1)
    packed = jnp.where(lane == 0, mean_here, jnp.where(lane == 1, square_here, 0.0))
    st[0] = jnp.transpose(packed)[0:8, :]

    pl.semaphore_wait(barrier, len(greeted))

    spread(0)
    tiles = st.at[1:NX]
    stat_copies = [
        cp.several(tiles, tiles, [(st.at[0], st.at[NX - d], xpeer(d)) for d in (2, 1, 3)])
    ]

    s0_a = [
        cp.remote(
            lat.at[pl.ds(pl.multiple_of(lax.rem(q + r, NQ) * rows, rows), rows), :], s0p, qpeer(r)
        )
        for r in range(1, NQ)
    ]

    @pl.when(tm == 0)
    def _():
        for c in s0_a:
            c.start()
        s0p[...] = lat[0:rows, :]

    for c in stat_copies:
        c.wait_recv()
    heard(0)
    spread(1)
    stats = [st[d] for d in range(NX)]
    mean_row = (stats[0][0:1] + stats[1][0:1] + stats[2][0:1] + stats[3][0:1]) / NX
    square_row = jnp.zeros_like(mean_row)
    for d in range(NX):
        shift = stats[d][0:1] - mean_row
        square_row += stats[d][1:2] + cols * (shift * shift)
    scale_row = lax.rsqrt(square_row / (cols * NX) + EPSILON)
    sub = lax.broadcasted_iota(jnp.int32, (128, tokens), 0)
    columns = jnp.transpose(jnp.where(sub == 0, mean_row, jnp.where(sub == 1, scale_row, 0.0)))
    mean_col, scale_col = columns[:, 0:1], columns[:, 1:2]
    load_mod.wait()
    deep = cols // 2

    def prepare(k):
        part = slice(k * deep, (k + 1) * deep)
        normed = (lat[:, part] - mean_col) * scale_col
        modin = normed * (1.0 + mod[1][:, part]) + mod[0][:, part]
        xin[0, k] = modin.astype(jnp.bfloat16)

    to_right = [cp.remote(xin.at[0, k], xin.at[3, k], xpeer(1)) for k in range(2)]
    to_left = [cp.remote(xin.at[0, k], xin.at[1, k], xpeer(3)) for k in range(2)]
    pass_right = cp.remote(xin.at[3, 0], xin.at[2, 0], xpeer(1))
    pass_left = cp.remote(xin.at[1, 1], xin.at[2, 1], xpeer(3))
    prepare(0)
    to_right[0].start()
    prepare(1)
    for c in (to_left[1], to_right[1], to_left[0]):
        c.start()

    lat_copies = []
    for r in range(1, NQ):
        there = pl.ds(pl.multiple_of(lax.rem(q + r, NQ) * rows, rows), rows)
        lat_copies.append((lat.at[there, :], latp.at[q], qpeer(r)))
    lat_copies = [cp.several(lat.at[0 : tokens - rows, :], latp.at[0 : NQ - 1], lat_copies)]
    latp[q] = lat[pl.ds(pl.multiple_of(q * rows, rows), rows), :]

    def project(d, k, first=False):
        for j in range(3):
            part = jnp.dot(
                xin[d, k], wq[d, j, k * deep : (k + 1) * deep, :],
                preferred_element_type=jnp.float32,
            )
            acc[j] = part if first else acc[j] + part

    load_wq[0].wait()
    project(0, 0, True)
    project(0, 1)
    to_right[0].wait_recv()
    pass_right.start()
    to_left[1].wait_recv()
    pass_left.start()
    heard(1)
    spread(2)
    load_wq[3].wait()
    project(3, 0)
    load_wq[1].wait()
    project(1, 1)
    heard(2)
    s0_b = [cp.remote(s0p, s0p, zpeer(r)) for r in range(1, NZ)]

    @pl.when(z == 0)
    def _():
        for i, c in enumerate(s0_a):

            @pl.when(q == i + 1)
            def _():
                c.wait_recv()

        for c in s0_b:
            c.start()

    to_right[1].wait_recv()
    project(3, 1)
    to_left[0].wait_recv()
    project(1, 0)
    load_wq[2].wait()
    pass_right.wait_recv()
    pass_left.wait_recv()
    for j in range(3):
        acc[j] += sum(
            jnp.dot(
                xin[2, k], wq[2, j, k * deep : (k + 1) * deep, :],
                preferred_element_type=jnp.float32,
            )
            for k in range(2)
        )

    places = [slice(h, h + HEAD) for h in range(0, heads.shape[1], HEAD)]

    def normal(j, here):
        t = acc[j, :, here]
        scale = lax.rsqrt(jnp.mean(t * t, axis=-1, keepdims=True) + EPSILON)
        return t * scale * gain_ref[j : j + 1, :]

    load_gain.wait()
    load_off.wait()
    pairs = [(normal(0, here), normal(1, here)) for here in places]
    scores = [
        lax.dot_general(
            a, b, (((1,), (1,)), ((), ())),
            precision=lax.Precision.HIGHEST, preferred_element_type=jnp.float32,
        ) * (HEAD ** -0.5)
        for a, b in pairs
    ]
    weights = [jnp.exp(t - jnp.max(t, axis=-1, keepdims=True)) for t in scores]
    probs = [(t / jnp.sum(t, axis=-1, keepdims=True)).astype(jnp.bfloat16) for t in weights]
    for here, t in zip(places, probs):
        values = acc[2, :, here].astype(jnp.bfloat16)
        heads[:, here] = jnp.dot(t, values, preferred_element_type=jnp.float32).astype(
            jnp.bfloat16
        )

    for load in load_wo:
        load.wait()
    part_copies = []
    for p in range(PARTS):
        at = slice(p * half, (p + 1) * half)
        copies = {}
        for d in (2, 1, 3):
            psend[p, d] = jnp.dot(
                heads[...], wo[d, :, at], preferred_element_type=jnp.float32
            ).astype(jnp.bfloat16)
            copies[d] = cp.remote(psend.at[p, d], precv.at[p, NX - d], xpeer(d))
            copies[d].start()
        part_copies.append(copies)

    @pl.when(z != 0)
    def _():
        for i, c in enumerate(s0_b):

            @pl.when(z == i + 1)
            def _():
                c.wait_recv()

    mine = pl.ds(pl.multiple_of(q * rows, rows), rows)
    most = s0.at[0 : tokens - rows, :]
    s0_c = [
        cp.several(most, most, [(s0p, s0.at[mine, :], qpeer(r)) for r in range(1, NQ)])
    ]
    s0[mine, :] = s0p[...]

    position = (off_ref[0] + tm).astype(jnp.float32)

    def noise_level(at):
        fraction = 1.0 - jnp.full((8, 128), at, jnp.float32) / (3.0 * NQ * NZ)
        return 3.0 * fraction / (1.0 + 2.0 * fraction)

    step_size = (noise_level(position + 1.0) - noise_level(position))[0:1, 0:1]

    step_ref[...] = jnp.broadcast_to(step_size, step_ref.shape)
    a_copies = []
    for p in range(PARTS):
        at = slice(p * half, (p + 1) * half)
        attended = jnp.dot(heads[...], wo[0, :, at], preferred_element_type=jnp.float32)
        for d in (1, 3, 2):
            part_copies[p][NX - d].wait_recv()
            attended += precv[p, d].astype(jnp.float32)
        gated = mod[2][:, at] * attended
        drift_ref[:, at] = gated
        drift_here = lat[:, at] + gated
        c_here = step_size * drift_here
        csend[p] = c_here.astype(jnp.bfloat16)
        copies = []
        for r in range(1, NQ):
            there = pl.ds(pl.multiple_of(lax.rem(q + r, NQ) * rows, rows), rows)
            copies.append((csend.at[p, there, :], arecv.at[p, q], qpeer(r)))
        others = pl.ds(0, tokens - rows)
        a_copies.append(cp.several(csend.at[p, others, :], arecv.at[p, 0 : NQ - 1], copies))
        arecv[p, q] = csend[p, mine, :]

    b_copies = []
    for p in range(PARTS):
        a_copies[p].wait_recv()
        total = jnp.zeros((rows, half), jnp.float32)
        for i in range(NQ):
            csum[p, i] = total
            total += arecv[p, i].astype(jnp.float32)
        bsend[p] = total.astype(jnp.bfloat16)
        copies = []
        for r in range(1, NZ):
            copies.append(cp.remote(bsend.at[p], brecv.at[p, r], zpeer(r)))

            @pl.when(z + r < NZ)
            def _():
                copies[-1].start()

        b_copies.append(copies)

    sent = stat_copies + to_right + to_left + [pass_right, pass_left] + lat_copies + s0_c
    for copies in part_copies:
        sent += list(copies.values())
    sent += a_copies
    for c in sent:
        c.wait_send()

    @pl.when(tm == 0)
    def _():
        for c in s0_a:
            c.wait_send()

    @pl.when(z == 0)
    def _():
        for c in s0_b:
            c.wait_send()

    for c in lat_copies:
        c.wait_recv()
    def send_squares():
        for i in range(NQ):
            tiles = [squares[i][:, b : b + 128] for b in range(0, half, 128)]
            rsend[i] = jnp.sum(sum(tiles[1:], tiles[0]), axis=0, keepdims=True)
        shares = rrecv.at[0 : len(near)]
        r_all = cp.several(
            shares, shares,
            [
                (rsend.at[lax.rem(q + r, NQ)], rrecv.at[n], xqpeer(d, r))
                for n, (d, r) in enumerate(near)
            ],
        )
        rrecv[len(near)] = rsend[q]
        return r_all

    c_copies = []
    squares = [jnp.zeros((rows, half), jnp.float32) for _ in range(NQ)]
    for p in range(PARTS):
        at = slice(p * half, (p + 1) * half)
        zsum[p] = jnp.zeros((rows, half), jnp.float32)
        for r in range(1, NZ):

            @pl.when(z >= r)
            def _():
                b_copies[p][r - 1].wait_recv()
                zsum[p] += brecv[p, r].astype(jnp.float32)

        before = zsum[p]
        for i in range(NQ):
            change = s0p[:, at] + (before + csum[p, i]) - latp[i, :, at]
            squares[i] += change * change
        if p == PARTS - 1:
            r_all = send_squares()
        for i in range(NQ):
            esend[p, i] = (before + csum[p, i]).astype(jnp.bfloat16)
        copies = [
            (esend.at[p, lax.rem(q + r, NQ)], erecv.at[p, mine, :], qpeer(r))
            for r in range(1, NQ)
        ]
        c_copies.append(cp.several(esend.at[p, 0 : NQ - 1], erecv.at[p, others, :], copies))
        erecv[p, mine, :] = esend[p, q]

    for c in s0_c:
        c.wait_recv()
    for c in c_copies + [r_all]:
        c.wait_send()

    for r in range(1, NZ):

        @pl.when(z + r < NZ)
        def _():
            for p in range(PARTS):
                b_copies[p][r - 1].wait_send()
    for p in range(PARTS):
        at = slice(p * half, (p + 1) * half)
        c_copies[p].wait_recv()
        upd_ref[:, at] = s0[:, at] + erecv[p].astype(jnp.float32)
    r_all.wait_recv()
    squared = jnp.sum(jnp.sum(rrecv[...], axis=0), axis=1, keepdims=True)
    res_ref[...] = squared / (tokens * cols * NX)


def body(starts, modulation, w_qkv, norm_gain, w_out, offset):
    tokens, cols = starts.shape[1:]
    inner = w_out.shape[0]
    half = cols // PARTS
    rows = tokens // NQ
    f32, bf16 = jnp.float32, jnp.bfloat16
    hbm = pl.BlockSpec(memory_space=pltpu.HBM)
    vmem = pl.BlockSpec(memory_space=pltpu.VMEM)
    fresh, gated, residual, step = pl.pallas_call(
        kernel,
        out_shape=(
            pltpu.VMEM((tokens, cols), f32),
            pltpu.VMEM((tokens, cols), f32),
            pltpu.VMEM((1, 1), f32),
            pltpu.VMEM((1, cols), f32),
        ),
        in_specs=[hbm, hbm, hbm, hbm, hbm, hbm],
        out_specs=(vmem, vmem, vmem, vmem),
        scratch_shapes=[
            pltpu.VMEM((tokens, cols), f32),
            pltpu.VMEM((3, 1, cols), f32),
            pltpu.SMEM((1,), jnp.int32),
            pltpu.VMEM((2, HEAD), f32),
            pltpu.VMEM((NX, 3, cols, inner), bf16),
            pltpu.VMEM((NX, inner, cols), bf16),
            pltpu.VMEM((NX, 8, 128), f32),
            pltpu.VMEM((NX, 2, tokens, cols // 2), bf16),
            pltpu.VMEM((3, tokens, inner), f32),
            pltpu.VMEM((tokens, inner), bf16),
            pltpu.VMEM((PARTS, NX, tokens, half), bf16),
            pltpu.VMEM((PARTS, NX, tokens, half), bf16),
            pltpu.VMEM((rows, cols), f32),
            pltpu.VMEM((tokens, cols), f32),
            pltpu.VMEM((PARTS, tokens, half), bf16),
            pltpu.VMEM((PARTS, NQ, rows, half), bf16),
            pltpu.VMEM((PARTS, rows, half), bf16),
            pltpu.VMEM((PARTS, NZ, rows, half), bf16),
            pltpu.VMEM((PARTS, NQ, rows, half), f32),
            pltpu.VMEM((PARTS, NQ, rows, half), bf16),
            pltpu.VMEM((PARTS, tokens, half), bf16),
            pltpu.VMEM((PARTS, rows, half), f32),
            pltpu.VMEM((NQ, rows, cols), f32),
            pltpu.VMEM((NQ, 1, 128), f32),
            pltpu.VMEM((NX * NQ, 1, 128), f32),
            pltpu.SemaphoreType.DMA((12,)),
            pltpu.SemaphoreType.DMA((REMOTE,)),
            pltpu.SemaphoreType.DMA((REMOTE,)),
            pltpu.SemaphoreType.REGULAR((3,)),
        ],
        compiler_params=pltpu.CompilerParams(
            collective_id=0, has_side_effects=True, vmem_limit_bytes=60 * 1024 * 1024
        ),
        name="sweep",
    )(
        starts.reshape(tokens, cols),
        modulation.transpose(1, 0, 2),
        w_qkv.transpose(1, 0, 2),
        norm_gain,
        w_out,
        offset,
    )
    drift = starts + gated[None]
    return (fresh[None] + step[None] * drift, drift, residual.reshape(1))


def solution(mesh):
    in_specs = (
        P("tm", None, "tp"),
        P("tm", None, None),
        P(None, None, "tp"),
        P(),
        P("tp", None),
        P(),
    )
    out_specs = (P("tm", None, "tp"), P("tm", None, "tp"), P("tm"))
    return jax.shard_map(body, mesh=mesh, in_specs=in_specs, out_specs=out_specs, check_vma=False)
```
